128 devices in a mesh: pool: 4 (over x), dev: 32 (over z, y, core).
Axes of the slice: x: 4, y: 4, z: 4, core: 2. Of those that a mesh axis runs over, the one named last changes fastest.
Arguments:
- patches: bfloat16 [256, 128, 1280], P('dev', 'pool'), may hold values from -6 to 6
- enc_tiles: int32 [32], replicated, may hold values from 1 to 8, 128 in all
- req_tiles: int32 [64], replicated, may hold values from 1 to 4, 128 in all
- req_owner: int32 [64, 1], replicated, may hold values from 0 to 3; in each aligned block of 64 rows (0 to 63, 64 to 127, ...) at most 24 rows name the same one
- fc1_weight: bfloat16 [1280, 5120], P(None, 'pool'), may hold values from -0.15625 to 0.15625
- fc2_weight: bfloat16 [5120, 1280], P('pool'), may hold values from -0.078125 to 0.078125
- key_weight: bfloat16 [1280, 1024], replicated, may hold values from -0.15625 to 0.15625
- value_weight: bfloat16 [1280, 1024], replicated, may hold values from -0.15625 to 0.15625
- query_weight: bfloat16 [8192, 8192], P(None, 'dev'), may hold values from -0.0625 to 0.0625
- out_weight: bfloat16 [8192, 8192], P('dev'), may hold values from -0.0625 to 0.0625
- text_hidden: bfloat16 [96, 4, 8192], P('pool'), may hold values from -6 to 6
Outputs:
- mixed: bfloat16 [96, 4, 8192], P('pool', None, 'dev')
The draws below stay inside these ranges and needn't reach their ends.
Inputs may be any that keep to these rules, and one draw needn't show every extreme that they name: `enc_tiles`: the entries sum to 128; the largest is 8. `req_tiles`: the entries sum to 128; the largest is 4. `req_owner`: no group owns more than 24 requests, and some group owns exactly 24.
All inputs are finite; a program needn't handle non-finite values.
Results may differ from the reference program's by a relative error of at most 0.008.
Values may be sent and summed in bfloat16 or wider, within the bound.
No kernel may reach another device: no remote copies, remote signals or barrier semaphores. Data moves between devices by JAX's collectives and lax.ppermute only.
A program may use at most 128 MiB of HBM per device.

```python
import math
import jax
import jax.numpy as jnp
import numpy as np
from jax import lax

VW = 1280
VFF = 5120
D = 8192
HEADS = 64
KV_HEADS = 8
HEAD_DIM = 128
PT = 128
STEPS = 4
MAXT = 4
ENC_CAP = 8
TILES = 128
REQUESTS = 64
R_CAP = 24
N_POOL = 4
N_DEV = 32


def steps_of(key, shape, shards, smallest, top_value):
    factor_of, own = 1.0, jax.random.fold_in(key, 6)
    for dim, shards_of in shards:
        steps = jnp.exp(jax.random.uniform(jax.random.fold_in(own, dim), (shards_of,), jnp.float32, smallest / len(shards), top_value / len(shards)))
        factor_of = factor_of * jnp.repeat(steps, shape[dim] // shards_of).reshape([-1 if axis == dim else 1 for axis in range(len(shape))])
    return factor_of


def split_up(count, total, bound, lean):
    loads = [(1 << 20) // math.isqrt(rank ** lean) + 1 for rank in range(2, count + 1)]
    spare, holding = total - bound - (count - 1), [1] * (count - 1)
    while spare > 0:
        candidates = [i for i in range(count - 1) if holding[i] < bound]
        mass, remaining = sum([loads[i] for i in candidates]), spare
        for i in candidates:
            addition = min(bound - holding[i], max(1, remaining * loads[i] // mass), spare)
            holding[i] = holding[i] + addition
            spare = spare - addition
    return np.array([bound] + holding)


def ragged_sizes(rng, amount, total, limit, skew):
    if amount == 2:
        one = jax.random.randint(rng, (), max(1, total - limit), min(limit, total - 1) + 1)
        return jnp.stack([one, total - one])
    tallies = jnp.asarray(split_up(amount, total, limit, skew), jnp.int32)
    pairs = (amount - 1) // 2
    giver, taker = tallies[1:1 + 2 * pairs:2], tallies[2:2 + 2 * pairs:2]
    room = jnp.minimum(giver - 1, limit - taker)
    shifted = jax.random.randint(jax.random.fold_in(rng, 1), (pairs,), 0, 1 << 20) % (room + 1)
    tallies = tallies.at[1:1 + 2 * pairs:2].set(giver - shifted).at[2:2 + 2 * pairs:2].set(taker + shifted)
    return tallies[jax.random.permutation(jax.random.fold_in(rng, 2), amount)]


def routed_block(key, own, number, rows, number_of, top, bound, slope):
    order = jax.random.permutation(key, number_of)
    packed, common = load_shares(number_of, rows * top, bound, slope, True), load_shares(number_of, rows * top, bound, slope, False)
    places = jnp.arange(number_of)

    def named(sizes, offset_by):
        used = int((sizes > 0).sum())
        fixed = max(1, used // 4)
        passed = fixed + (places - fixed + offset_by * (used - fixed)) % max(1, number_of - fixed)
        return jnp.zeros((number_of,), jnp.int32).at[order[jnp.where(places < fixed, places, passed)]].set(jnp.asarray(sizes, jnp.int32))

    sizes = jnp.where(number % 4 == 0, named(packed, number // 4), named(common, number - number // 4 - 1))
    mixed = jax.random.permutation(jax.random.fold_in(own, 3), number_of)
    donor, sink = mixed[0:number_of // 2 * 2:2], mixed[1:number_of // 2 * 2:2]
    margin = jnp.minimum(sizes[donor] - 1, bound - sizes[sink]) // 2
    margin = jnp.where((donor == order[0]) | (sink == order[0]) | (sizes[sink] == 0), 0, jnp.maximum(margin, 0))
    passed = jax.random.randint(jax.random.fold_in(own, 4), (number_of // 2,), 0, 1 << 20) % (margin + 1)
    sizes = sizes.at[donor].add(-passed).at[sink].add(passed)
    members = jnp.searchsorted(jnp.cumsum(sizes), jnp.arange(rows * top), side="right").astype(jnp.int32)
    grid = members.reshape(top, rows).T
    grid = grid[jax.random.permutation(jax.random.fold_in(own, 1), rows)]
    offset_by = jax.random.randint(jax.random.fold_in(own, 2), (rows, 1), 0, top)
    return jnp.take_along_axis(grid, (jnp.arange(top)[None, :] + offset_by) % top, axis=1)


def load_shares(amount, total, reach, skew, full):
    weights = [(1 << 20) // math.isqrt(rank ** skew) + 1 for rank in range(1, amount + 1)]
    largest = reach if full else min(reach, max(-(-total // amount), total * weights[0] // sum(weights)))
    least = 1 if total - largest >= amount - 1 else 0
    holding, surplus = [largest] + [least] * (amount - 1), total - largest - least * (amount - 1)
    while surplus > 0:
        movable = [i for i in range(1, amount) if holding[i] < largest] or [i for i in range(1, amount) if holding[i] < reach]
        whole, budget = sum([weights[i] for i in movable]), surplus
        for i in movable:
            more = min(reach - holding[i], max(1, budget * weights[i] // whole), surplus)
            holding[i] = holding[i] + more
            surplus = surplus - more
    return np.array(holding)


def bell_draw(key, dims, scale, most, shards=(), kind=jnp.bfloat16):
    drawn = jax.random.normal(key, dims, jnp.float32) * scale
    if len(shards) > 0:
        drawn = steps_of(key, dims, shards, -0.22, 0.18) * drawn
    return jnp.clip(drawn, min=-most, max=most).astype(kind)


def setup_inputs(seed: int = 0) -> dict:
    streams_of = jax.random.split(jax.random.key(seed), 12)
    patches = bell_draw(streams_of[0], (N_DEV * ENC_CAP, PT, VW), 1.0, 6.0, ((0, 32), (1, 4)))
    enc_tiles = ragged_sizes(streams_of[1], N_DEV, TILES, ENC_CAP, 2).astype(jnp.int32)
    req_tiles = ragged_sizes(streams_of[2], REQUESTS, TILES, MAXT, 1).astype(jnp.int32)
    req_owner_keys = jax.random.split(jax.random.fold_in(streams_of[3], 1), REQUESTS // REQUESTS)
    req_owner_turns = jax.random.permutation(jax.random.fold_in(streams_of[3], 3), REQUESTS // REQUESTS)
    req_owner = jax.vmap(lambda own, number: routed_block(jax.random.fold_in(streams_of[3], 2), own, number, REQUESTS, N_POOL, 1, R_CAP, 1))(req_owner_keys, req_owner_turns).reshape((REQUESTS, 1))
    fc1_weight = bell_draw(streams_of[4], (VW, VFF), VW ** -0.5, 0.15625, ((1, 4),))
    fc2_weight = bell_draw(streams_of[5], (VFF, VW), VFF ** -0.5, 0.078125, ((0, 4),))
    key_weight = bell_draw(streams_of[6], (VW, KV_HEADS * HEAD_DIM), VW ** -0.5, 0.15625)
    value_weight = bell_draw(streams_of[7], (VW, KV_HEADS * HEAD_DIM), VW ** -0.5, 0.15625)
    query_weight = bell_draw(streams_of[8], (D, HEADS * HEAD_DIM), D ** -0.5, 0.0625, ((1, 32),))
    out_weight = bell_draw(streams_of[9], (HEADS * HEAD_DIM, D), (HEADS * HEAD_DIM) ** -0.5, 0.0625, ((0, 32),))
    text_hidden = bell_draw(streams_of[10], (N_POOL * R_CAP, STEPS, D), 1.0, 6.0, ((0, 4),))
    return {"patches": patches, "enc_tiles": enc_tiles, "req_tiles": req_tiles, "req_owner": req_owner, "fc1_weight": fc1_weight, "fc2_weight": fc2_weight, "key_weight": key_weight, "value_weight": value_weight, "query_weight": query_weight, "out_weight": out_weight, "text_hidden": text_hidden}


epsilon = 1e-05

def layer_stats(values_in):
    center = values_in - lax.optimization_barrier(jnp.mean(values_in, axis=-1, keepdims=True))
    spread = lax.optimization_barrier(jnp.mean(center * center, axis=-1, keepdims=True))
    return center / jnp.sqrt(spread + epsilon)

def rms_scale(values_in):
    return values_in / jnp.sqrt(lax.optimization_barrier(jnp.mean(values_in * values_in, axis=-1, keepdims=True)) + epsilon)

def slot_tables(enc_tiles, req_tiles, req_owner, groups, slots, capacity, most_tiles):
    enc_start = (jnp.cumsum(enc_tiles) - enc_tiles).astype(jnp.int32)
    req_start = (jnp.cumsum(req_tiles) - req_tiles).astype(jnp.int32)
    owner = req_owner[:, 0]
    group_ids = jnp.arange(groups, dtype=jnp.int32)
    member = (owner[:, None] == group_ids[None, :]).astype(jnp.int32)
    rank_in = lax.optimization_barrier(jnp.sum((jnp.cumsum(member, axis=0).astype(jnp.int32) - 1) * member, axis=1)).astype(jnp.int32)
    slot_ids = jnp.arange(slots, dtype=jnp.int32)
    match = ((owner[None, None, :] == group_ids[:, None, None]) & (rank_in[None, None, :] == slot_ids[None, :, None])).astype(jnp.int32)
    live = lax.optimization_barrier(jnp.sum(match, axis=2)) > 0
    length = lax.optimization_barrier(jnp.sum(match * req_tiles[None, None, :], axis=2)).astype(jnp.int32)
    first_tile = lax.optimization_barrier(jnp.sum(match * req_start[None, None, :], axis=2)).astype(jnp.int32)
    position = jnp.arange(most_tiles, dtype=jnp.int32)
    valid = position[None, None, :] < length[:, :, None]
    tile_index = first_tile[:, :, None] + position[None, None, :]
    column = (lax.optimization_barrier(jnp.sum((enc_start <= tile_index[..., None]).astype(jnp.int32), axis=-1)) - 1).astype(jnp.int32)
    column_hit = (column[..., None] == jnp.arange(enc_tiles.shape[0], dtype=jnp.int32)).astype(jnp.int32)
    column_start = lax.optimization_barrier(jnp.sum(column_hit * enc_start, axis=-1)).astype(jnp.int32)
    source = column * capacity + tile_index - column_start
    source = jnp.where(valid, source, 0).astype(jnp.int32)
    return (source, valid, live)

def reference(patches, enc_tiles, req_tiles, req_owner, fc1_weight, fc2_weight, key_weight, value_weight, query_weight, out_weight, text_hidden):
    columns = patches.reshape(N_DEV, ENC_CAP * PT, VW)

    def encode_column(column_rows):
        normed = layer_stats(column_rows.astype(jnp.float32)).astype(jnp.bfloat16)
        widened = jax.nn.gelu(jnp.dot(normed, fc1_weight, preferred_element_type=jnp.float32), approximate=False).astype(jnp.bfloat16)
        vision = (column_rows.astype(jnp.float32) + jnp.dot(widened, fc2_weight, preferred_element_type=jnp.float32)).astype(jnp.bfloat16)
        key_rows = rms_scale(jnp.dot(vision, key_weight, preferred_element_type=jnp.float32).reshape(ENC_CAP * PT, KV_HEADS, HEAD_DIM)).astype(jnp.bfloat16)
        value_rows = jnp.dot(vision, value_weight, preferred_element_type=jnp.float32).astype(jnp.bfloat16).reshape(ENC_CAP * PT, KV_HEADS, HEAD_DIM)
        return jnp.concatenate([key_rows, value_rows], axis=-1)
    kv_table = lax.map(encode_column, columns).reshape(N_DEV * ENC_CAP, PT, KV_HEADS, 2 * HEAD_DIM)
    source, valid, live = slot_tables(enc_tiles, req_tiles, req_owner, N_POOL, R_CAP, ENC_CAP, MAXT)
    scale = HEAD_DIM ** (-0.5)
    group_size = HEADS // KV_HEADS

    def decode_slot(inputs):
        hidden, slot_source, slot_valid, slot_live = inputs
        normed = rms_scale(hidden.astype(jnp.float32)).astype(jnp.bfloat16)
        query = jnp.dot(normed, query_weight, preferred_element_type=jnp.float32).reshape(STEPS, KV_HEADS, group_size, HEAD_DIM)
        query = rms_scale(query).astype(jnp.bfloat16)
        tiles = kv_table[slot_source]
        key_part = tiles[..., :HEAD_DIM].astype(jnp.float32)
        value_part = tiles[..., HEAD_DIM:].astype(jnp.float32)
        scores = jnp.einsum('sgqd,mngd->sgqmn', query.astype(jnp.float32), key_part) * scale
        weights = jnp.exp(scores) * slot_valid.astype(jnp.float32)[:, None]
        total = lax.optimization_barrier(jnp.sum(weights, axis=(3, 4)))
        total = jnp.where(slot_live, total, jnp.ones_like(total))
        weights = (weights / total[..., None, None]).astype(jnp.bfloat16)
        attended = jnp.einsum('sgqmn,mngd->sgqd', weights.astype(jnp.float32), value_part).astype(jnp.bfloat16)
        update = jnp.dot(attended.reshape(STEPS, HEADS * HEAD_DIM), out_weight, preferred_element_type=jnp.float32)
        return (hidden.astype(jnp.float32) + update).astype(jnp.bfloat16)
    return lax.map(decode_slot, (text_hidden, source.reshape(N_POOL * R_CAP, MAXT), valid.reshape(N_POOL * R_CAP, MAXT), live.reshape(N_POOL * R_CAP)))
```

```python
import jax
import jax.numpy as jnp
from jax import lax
from jax.sharding import PartitionSpec as P

HEADS = 64
KV_HEADS = 8
HEAD_DIM = 128
MAXT = 4
CORES = 2
RING = 4


epsilon = 1e-05


def layer_stats(values_in):
    center = values_in - jnp.mean(values_in, axis=-1, keepdims=True)
    spread = jnp.mean(center * center, axis=-1, keepdims=True)
    return center / jnp.sqrt(spread + epsilon)


def rms_scale(values_in):
    return values_in / jnp.sqrt(jnp.mean(values_in * values_in, axis=-1, keepdims=True) + epsilon)


def slot_tables(enc_tiles, req_tiles, req_owner, groups, slots, capacity, most_tiles):
    enc_start = jnp.cumsum(enc_tiles) - enc_tiles
    req_start = jnp.cumsum(req_tiles) - req_tiles
    owner = req_owner[:, 0]
    group_ids = jnp.arange(groups, dtype=jnp.int32)
    member = (owner[:, None] == group_ids[None, :]).astype(jnp.int32)
    rank_in = jnp.sum((jnp.cumsum(member, axis=0) - 1) * member, axis=1)
    slot_ids = jnp.arange(slots, dtype=jnp.int32)
    match = (
        (owner[None, None, :] == group_ids[:, None, None])
        & (rank_in[None, None, :] == slot_ids[None, :, None])
    ).astype(jnp.int32)
    live = jnp.sum(match, axis=2) > 0
    length = jnp.sum(match * req_tiles[None, None, :], axis=2)
    first_tile = jnp.sum(match * req_start[None, None, :], axis=2)
    position = jnp.arange(most_tiles, dtype=jnp.int32)
    valid = position[None, None, :] < length[:, :, None]
    tile_index = first_tile[:, :, None] + position[None, None, :]
    column = jnp.sum((enc_start <= tile_index[..., None]).astype(jnp.int32), axis=-1) - 1
    column_hit = (column[..., None] == jnp.arange(enc_tiles.shape[0], dtype=jnp.int32)).astype(
        jnp.int32
    )
    column_start = jnp.sum(column_hit * enc_start, axis=-1)
    source = column * capacity + tile_index - column_start
    source = jnp.where(valid, source, 0)
    return (source, valid, live)


def pool_shift(x, by):
    return lax.ppermute(x, "pool", [(i, (i + by) % RING) for i in range(RING)])


def dev_shift(x, by_z, by_y, by_core):
    pairs = []
    for z in range(RING):
        for y in range(RING):
            for k in range(CORES):
                to = ((z + by_z) % RING, (y + by_y) % RING, (k + by_core) % CORES)
                pairs.append(((z * RING + y) * CORES + k, (to[0] * RING + to[1]) * CORES + to[2]))
    return lax.ppermute(x, "dev", pairs)


def feed_forward(rows, fc1_weight, fc2_weight):
    widened = jax.nn.gelu(
        jnp.dot(rows, fc1_weight, preferred_element_type=jnp.float32), approximate=False
    ).astype(jnp.bfloat16)
    return jnp.dot(widened, fc2_weight, preferred_element_type=jnp.float32)


def body(
    patches,
    enc_tiles,
    req_tiles,
    req_owner,
    fc1_weight,
    fc2_weight,
    key_weight,
    value_weight,
    query_weight,
    out_weight,
    text_hidden,
):
    capacity, quarter, width_in = patches.shape
    groups = lax.axis_size("pool")
    devices = lax.axis_size("dev")
    local_heads = HEADS // devices
    slots, steps, model_width = text_hidden.shape
    pool_at = lax.axis_index("pool")
    dev_at = lax.axis_index("dev")
    halves = capacity // RING
    rows = RING * quarter
    f32, bf16 = jnp.float32, jnp.bfloat16

    order = (pool_at + jnp.arange(RING)) % RING
    own_raw, own_rows = [], []
    for i in range(halves):
        part = jnp.take(patches[i * RING : (i + 1) * RING], order, axis=0).reshape(rows, width_in)
        own_raw.append(part)
        own_rows.append(layer_stats(part.astype(f32)).astype(bf16))

    normed_text = (
        rms_scale(text_hidden.astype(f32)).astype(bf16).reshape(slots * steps, model_width)
    )
    query = jnp.dot(normed_text, query_weight, preferred_element_type=f32).reshape(
        slots, steps * local_heads, HEAD_DIM
    )
    query = rms_scale(query).astype(bf16).reshape(slots, steps * local_heads * HEAD_DIM)
    by_offset = jnp.stack([query] + [pool_shift(query, s) for s in range(1, RING)])
    all_queries = jnp.take(by_offset, (pool_at - jnp.arange(groups)) % RING, axis=0).reshape(
        groups * slots, steps * local_heads * HEAD_DIM
    )
    source, valid, live = slot_tables(
        enc_tiles, req_tiles, req_owner, groups, slots, capacity, MAXT
    )
    held = (
        jnp.arange(devices)[:, None] * capacity + jnp.arange(halves)[None, :] * RING + pool_at
    ).reshape(-1)
    holds = jnp.sum(
        (
            (source.reshape(groups * slots, MAXT, 1) == held)
            & valid.reshape(groups * slots, MAXT, 1)
        ).astype(f32),
        axis=1,
    ).astype(bf16)
    tile_queries = lax.dot_general(
        holds, all_queries, (((0,), (0,)), ((), ())), preferred_element_type=f32
    ).astype(bf16)
    tile_queries = lax.all_to_all(
        tile_queries.reshape(devices, halves, steps * local_heads * HEAD_DIM),
        "dev",
        split_axis=0,
        concat_axis=0,
        tiled=True,
    )
    heads_per_group = HEADS // KV_HEADS
    tile_queries = jnp.transpose(
        tile_queries.reshape(
            KV_HEADS, devices // KV_HEADS, halves, steps * local_heads, HEAD_DIM
        ),
        (2, 0, 1, 3, 4),
    ).reshape(halves, KV_HEADS, heads_per_group * steps, HEAD_DIM)

    numerators, totals = [], []
    for i in range(halves):
        half_rows = rows // 2
        from_left = pool_shift(own_rows[i], 1)
        from_right = pool_shift(own_rows[i], -1)
        far = jnp.concatenate(
            [pool_shift(from_left[:half_rows], 1), pool_shift(from_right[half_rows:], -1)], axis=0
        )
        outs = [
            feed_forward(own_rows[i], fc1_weight, fc2_weight) + own_raw[i].astype(f32),
            feed_forward(from_left, fc1_weight, fc2_weight),
            feed_forward(far, fc1_weight, fc2_weight),
            feed_forward(from_right, fc1_weight, fc2_weight),
        ]
        outs = [o.reshape(RING, quarter, width_in) for o in outs]
        total = jnp.stack([outs[m][m] for m in range(RING)])
        for s in range(1, RING):
            message = jnp.stack([outs[(m - s) % RING][m] for m in range(RING)]).astype(bf16)
            total = total + pool_shift(message, s).astype(f32)
        vision = total.astype(bf16).reshape(rows, width_in)
        key_rows = rms_scale(
            jnp.dot(vision, key_weight, preferred_element_type=f32).reshape(
                rows, KV_HEADS, HEAD_DIM
            )
        ).astype(bf16)
        value_rows = (
            jnp.dot(vision, value_weight, preferred_element_type=f32)
            .astype(bf16)
            .reshape(rows, KV_HEADS, HEAD_DIM)
        )
        scores = jnp.einsum(
            "hqd,nhd->hqn", tile_queries[i], key_rows, preferred_element_type=f32
        ) * HEAD_DIM ** (-0.5)
        weights = jnp.exp(scores)
        totals.append(jnp.sum(weights, axis=-1))
        numerators.append(
            jnp.einsum(
                "hqn,nhd->hqd", weights.astype(bf16), value_rows, preferred_element_type=f32
            )
        )
    numerator = jnp.stack(numerators).reshape(
        halves, devices, steps * local_heads, HEAD_DIM
    )
    total = jnp.broadcast_to(
        jnp.stack(totals).reshape(halves, devices, steps * local_heads, 1), numerator.shape
    )
    partial = jnp.concatenate([numerator, total], axis=-1).astype(bf16)
    partial = lax.all_to_all(
        jnp.transpose(partial, (1, 0, 2, 3)), "dev", split_axis=0, concat_axis=0, tiled=True
    ).reshape(devices * halves, steps * local_heads * 2 * HEAD_DIM)
    combined = jnp.dot(holds, partial, preferred_element_type=f32).reshape(
        groups, slots, steps * local_heads, 2 * HEAD_DIM
    )
    combined = jnp.take(combined, order, axis=0)
    attended = combined[0]
    for s in range(1, RING):
        attended = attended + pool_shift(combined[s].astype(bf16), s).astype(f32)
    slot_live = lax.dynamic_index_in_dim(live, pool_at, 0, keepdims=False)
    divisor = jnp.where(slot_live[:, None, None], attended[..., HEAD_DIM:], 1.0)
    attended = (attended[..., :HEAD_DIM] / divisor).astype(bf16)

    width_out = model_width // devices
    partial_out = jnp.dot(
        attended.reshape(slots * steps, local_heads * HEAD_DIM),
        out_weight,
        preferred_element_type=f32,
    ).astype(bf16)
    z_at, y_at, core_at = dev_at // (RING * CORES), (dev_at // CORES) % RING, dev_at % CORES
    core_r, z_r, y_r = jnp.meshgrid(
        jnp.arange(CORES), jnp.arange(RING), jnp.arange(RING), indexing="ij"
    )
    blocks = (
        ((z_at + z_r) % RING * RING + (y_at + y_r) % RING) * CORES + (core_at + core_r) % CORES
    ).reshape(-1)
    by_block = jnp.transpose(
        partial_out.reshape(slots * steps, devices, width_out), (1, 0, 2)
    )
    by_block = jnp.take(by_block, blocks, axis=0).reshape(
        CORES, RING, RING, slots * steps, width_out
    )
    kept = by_block[0].astype(f32) + dev_shift(by_block[1], 0, 0, 1).astype(f32)
    rounded = kept.astype(bf16)
    kept = kept[0]
    for s in range(1, RING):
        kept = kept + dev_shift(rounded[s], s, 0, 0).astype(f32)
    rounded = kept.astype(bf16)
    kept = kept[0]
    for s in range(1, RING):
        kept = kept + dev_shift(rounded[s], 0, s, 0).astype(f32)
    residual = lax.dynamic_slice_in_dim(text_hidden, dev_at * width_out, width_out, 2)
    mixed = (residual.reshape(slots * steps, width_out).astype(f32) + kept).astype(bf16)
    return mixed.reshape(slots, steps, width_out)


def solution(mesh):
    return jax.shard_map(
        body,
        mesh=mesh,
        in_specs=(
            P("dev", "pool", None),
            P(),
            P(),
            P(),
            P(None, "pool"),
            P("pool", None),
            P(),
            P(),
            P(None, "dev"),
            P("dev", None),
            P("pool", None, None),
        ),
        out_specs=P("pool", None, "dev"),
        check_vma=False,
    )
```

```python
import functools

import jax
import jax.numpy as jnp
from jax import lax
from jax.experimental import pallas as pl
from jax.experimental.pallas import tpu as pltpu
from jax.sharding import PartitionSpec as P

HEADS = 64
KV_HEADS = 8
HEAD_DIM = 128
CORES = 2
RING = 4
BLOCK = 256
F32, BF16 = jnp.float32, jnp.bfloat16

epsilon = 1e-05

VMEM = pl.BlockSpec(memory_space=pltpu.VMEM)
SMEM = pl.BlockSpec(memory_space=pltpu.SMEM)


def params(mib):
    return pltpu.CompilerParams(vmem_limit_bytes=mib * 1024 * 1024)


def pool_shift(x, by):
    return lax.ppermute(x, "pool", [(i, (i + by) % RING) for i in range(RING)])


def dev_shift(x, by_z, by_y, by_core):
    pairs = []
    for z in range(RING):
        for y in range(RING):
            for k in range(CORES):
                to = ((z + by_z) % RING, (y + by_y) % RING, (k + by_core) % CORES)
                pairs.append(((z * RING + y) * CORES + k, (to[0] * RING + to[1]) * CORES + to[2]))
    return lax.ppermute(x, "dev", pairs)


def normalize_kernel(half, at_ref, patches_ref, rows_ref):
    for r in range(RING):
        slot = lax.rem(at_ref[0] + r, RING) + half * RING
        values = patches_ref[slot].astype(F32)
        center = values - jnp.mean(values, axis=-1, keepdims=True)
        spread = jnp.mean(center * center, axis=-1, keepdims=True)
        rows_ref[r] = (center / jnp.sqrt(spread + epsilon)).astype(BF16)


def normalize(at, patches, half):
    _, quarter, width = patches.shape
    return pl.pallas_call(
        functools.partial(normalize_kernel, half),
        out_shape=jax.ShapeDtypeStruct((RING, quarter, width), BF16),
        in_specs=[SMEM, VMEM],
        out_specs=VMEM,
        compiler_params=params(16),
    )(at, patches)


def feed_forward_kernel(
    half, quarter, at_ref, patches_ref, own_ref, left_ref, right_ref, far_left_ref, far_right_ref,
    fc1_ref, fc2_ref, total_ref, one_ref, two_ref, three_ref, rows_ref, wide_ref,
):
    width, hidden = fc1_ref.shape
    rows = RING * quarter
    for at, ref in ((0, own_ref), (1, left_ref), (3, right_ref)):
        rows_ref[at * rows : (at + 1) * rows] = ref[...].reshape(rows, width)
    rows_ref[2 * rows : 2 * rows + rows // 2] = far_left_ref[...].reshape(rows // 2, width)
    rows_ref[2 * rows + rows // 2 : 3 * rows] = far_right_ref[...].reshape(rows // 2, width)

    def widen(step, _):
        at = pl.ds(pl.multiple_of(step * BLOCK, BLOCK), BLOCK)
        values = jnp.dot(rows_ref[...], fc1_ref[:, at], preferred_element_type=F32)
        wide_ref[:, at] = (0.5 * values * (1.0 + lax.erf(values * 0.5**0.5))).astype(BF16)
        return 0

    lax.fori_loop(0, hidden // BLOCK, widen, 0)
    outs = (total_ref, one_ref, two_ref, three_ref)

    def narrow(step, _):
        at = pl.ds(pl.multiple_of(step * BLOCK, BLOCK), BLOCK)
        sums = jnp.dot(wide_ref[...], fc2_ref[:, at], preferred_element_type=F32)
        for source in range(RING):
            for m in range(RING):
                piece = sums[source * rows + m * quarter : source * rows + (m + 1) * quarter]
                shift = (m - source) % RING
                if source == 0:
                    slot = lax.rem(at_ref[0] + m, RING) + half * RING
                    piece = piece + patches_ref[slot, :, at].astype(F32)
                outs[shift][m, :, at] = piece.astype(outs[shift].dtype)
        return 0

    lax.fori_loop(0, width // BLOCK, narrow, 0)


def feed_forward(at, patches, own, left, right, far_left, far_right, fc1, fc2, half):
    _, quarter, width = patches.shape
    hidden = fc1.shape[1]
    shape = (RING, quarter, width)
    sent = jax.ShapeDtypeStruct(shape, BF16)
    return pl.pallas_call(
        functools.partial(feed_forward_kernel, half, quarter),
        out_shape=(jax.ShapeDtypeStruct(shape, F32), sent, sent, sent),
        in_specs=[SMEM] + [VMEM] * 8,
        out_specs=(VMEM,) * 4,
        scratch_shapes=[
            pltpu.VMEM((RING * RING * quarter, width), BF16),
            pltpu.VMEM((RING * RING * quarter, hidden), BF16),
        ],
        compiler_params=params(32),
        cost_estimate=pl.CostEstimate(
            flops=4 * RING * RING * quarter * width * hidden,
            bytes_accessed=4 * width * hidden,
            transcendentals=0,
        ),
    )(at, patches, own, left, right, far_left, far_right, fc1, fc2)


def query_kernel(text_ref, weight_ref, query_ref, total_ref, square_ref):
    step = pl.program_id(0)

    @pl.when(step == 0)
    def _():
        total_ref[...] = jnp.zeros_like(total_ref)
        square_ref[...] = jnp.zeros_like(square_ref)

    text = text_ref[...]
    total_ref[...] += jnp.dot(text, weight_ref[...], preferred_element_type=F32)
    wide = text.astype(F32)
    square_ref[...] += jnp.sum(wide * wide, axis=-1, keepdims=True)

    @pl.when(step == pl.num_programs(0) - 1)
    def _():
        width = text_ref.shape[1] * pl.num_programs(0)
        values = total_ref[...] / jnp.sqrt(square_ref[...] / width + epsilon)
        for head in range(query_ref.shape[0]):
            part = values[:, head * HEAD_DIM : (head + 1) * HEAD_DIM]
            mean = jnp.mean(part * part, axis=-1, keepdims=True)
            query_ref[head] = (part / jnp.sqrt(mean + epsilon)).astype(BF16)


def make_query(text, weight):
    rows, width = text.shape
    columns = weight.shape[1]
    depth = 2048
    return pl.pallas_call(
        query_kernel,
        grid=(width // depth,),
        out_shape=jax.ShapeDtypeStruct((columns // HEAD_DIM, rows, HEAD_DIM), BF16),
        in_specs=[
            pl.BlockSpec((rows, depth), lambda k: (0, k)),
            pl.BlockSpec((depth, columns), lambda k: (k, 0)),
        ],
        out_specs=pl.BlockSpec((columns // HEAD_DIM, rows, HEAD_DIM), lambda k: (0, 0, 0)),
        scratch_shapes=[pltpu.VMEM((rows, columns), F32), pltpu.VMEM((rows, 1), F32)],
        compiler_params=params(16),
        cost_estimate=pl.CostEstimate(
            flops=2 * rows * width * columns,
            bytes_accessed=2 * width * (columns + rows),
            transcendentals=0,
        ),
    )(text, weight)


def iota(shape, dim):
    return lax.broadcasted_iota(jnp.int32, shape, dim)


def select_kernel(
    slots, steps, heads, capacity, at_ref, enc_ref, req_ref, owner_ref,
    own_ref, one_ref, two_ref, three_ref, chosen_ref, target_ref,
):
    here = at_ref[0]
    columns, requests = enc_ref.shape[1], req_ref.shape[1]
    halves = capacity // RING
    per_group = heads * slots * steps
    rows = columns * halves * heads * steps
    before = iota((requests, requests), 0) < iota((requests, requests), 1)
    equal = iota((requests, requests), 0) == iota((requests, requests), 1)
    req_row = req_ref[...]
    req_column = jnp.sum(jnp.where(equal, req_row, 0), axis=1, keepdims=True)
    req_start = jnp.sum(jnp.where(before, req_column, 0), axis=0, keepdims=True)
    owner_column = owner_ref[...]
    owner_row = jnp.sum(jnp.where(equal, owner_column, 0), axis=0, keepdims=True)
    rank = jnp.sum(
        jnp.where(before & (owner_column == owner_row), 1, 0), axis=0, keepdims=True
    )
    place = owner_row * per_group + rank * steps
    enc_row = enc_ref[...]
    enc_equal = iota((columns, columns), 0) == iota((columns, columns), 1)
    enc_before = iota((columns, columns), 0) < iota((columns, columns), 1)
    enc_column = jnp.sum(jnp.where(enc_equal, enc_row, 0), axis=1, keepdims=True)
    enc_start = jnp.sum(jnp.where(enc_before, enc_column, 0), axis=0, keepdims=True)

    row = iota((rows, 1), 0)
    per_tile = heads * steps
    column = row // (halves * per_tile)
    slot = row // per_tile % halves * RING + here
    hit = column == iota((rows, columns), 1)
    count = jnp.sum(jnp.where(hit, enc_row, 0), axis=1, keepdims=True)
    start = jnp.sum(jnp.where(hit, enc_start, 0), axis=1, keepdims=True)
    tile = jnp.where(slot < count, start + slot, -1)
    has = (req_start <= tile) & (tile < req_start + req_row)
    base = jnp.sum(jnp.where(has, place + 1, 0), axis=1, keepdims=True) - 1
    within = row % per_tile
    target = jnp.where(base < 0, -1, base + within // steps * (slots * steps) + within % steps)
    target_ref[...] = target
    chosen = jnp.zeros((rows, HEAD_DIM), F32)
    for shift, ref in enumerate((own_ref, one_ref, two_ref, three_ref)):
        group = lax.rem(here - shift + RING, RING)
        match = target == iota((rows, per_group), 1) + group * per_group
        chosen = chosen + jnp.dot(
            jnp.where(match, 1.0, 0.0).astype(BF16),
            ref[...].reshape(per_group, HEAD_DIM),
            preferred_element_type=F32,
        )
    chosen_ref[...] = chosen.astype(BF16)


def select(at, enc, req, owner, queries, slots, steps, capacity):
    heads = queries[0].shape[0]
    rows = enc.shape[1] * (capacity // RING) * heads * steps
    return pl.pallas_call(
        functools.partial(select_kernel, slots, steps, heads, capacity),
        out_shape=(
            jax.ShapeDtypeStruct((rows, HEAD_DIM), BF16),
            jax.ShapeDtypeStruct((rows, 1), jnp.int32),
        ),
        in_specs=[SMEM] + [VMEM] * 7,
        out_specs=(VMEM, VMEM),
        compiler_params=params(16),
    )(at, enc, req, owner, *queries)


def attend_kernel(half, first, quarter, *refs):
    if first:
        total_ref, one_ref, two_ref, three_ref, key_ref, value_ref, query_ref, out_ref, vision = refs
    else:
        (total_ref, one_ref, two_ref, three_ref, key_ref, value_ref, query_ref, before_ref,
         out_ref, vision) = refs
    rows = RING * quarter

    @pl.when(pl.program_id(0) == 0)
    def _():
        summed = total_ref[...]
        for ref in (one_ref, two_ref, three_ref):
            summed = summed + ref[...].astype(F32)
        vision[...] = summed.astype(BF16).reshape(rows, vision.shape[1])

    keys = jnp.dot(vision[...], key_ref[...], preferred_element_type=F32)
    values = jnp.dot(vision[...], value_ref[...], preferred_element_type=F32).astype(BF16)
    per_head, per_device = query_ref.shape[1], query_ref.shape[2]
    count = per_head * per_device
    mine = iota((count, 1), 0) % per_device // (per_device // 2) == half
    for head in range(query_ref.shape[0]):
        at = slice(head * HEAD_DIM, (head + 1) * HEAD_DIM)
        key = keys[:, at]
        mean = jnp.mean(key * key, axis=-1, keepdims=True)
        key = (key / jnp.sqrt(mean + epsilon)).astype(BF16)
        query = query_ref[head].reshape(count, HEAD_DIM)
        scores = lax.dot_general(
            query, key, (((1,), (1,)), ((), ())), preferred_element_type=F32
        ) * HEAD_DIM ** (-0.5)
        weights = jnp.where(mine, jnp.exp(scores), 0.0)
        divisor = jnp.sum(weights, axis=-1, keepdims=True)
        numerator = jnp.dot(weights.astype(BF16), values[:, at], preferred_element_type=F32)
        packed = jnp.concatenate(
            [numerator, jnp.broadcast_to(divisor, numerator.shape)], axis=1
        ).reshape(per_head, per_device, 2 * HEAD_DIM)
        if not first:
            packed = packed + before_ref[head].astype(F32)
        out_ref[head] = packed.astype(BF16)


def attend(total, received, key_weight, value_weight, queries, half, before):
    _, quarter, width = total.shape
    heads, per_head, per_device, _ = queries.shape
    columns = key_weight.shape[1]
    grid = 4
    each = heads // grid
    sums = pl.BlockSpec((RING, quarter, width), lambda h: (0, 0, 0))
    weight = pl.BlockSpec((width, columns // grid), lambda h: (0, h))
    packed = pl.BlockSpec((each, per_head, per_device, 2 * HEAD_DIM), lambda h: (h, 0, 0, 0))
    first = before is None
    return pl.pallas_call(
        functools.partial(attend_kernel, half, first, quarter),
        grid=(grid,),
        out_shape=jax.ShapeDtypeStruct((heads, per_head, per_device, 2 * HEAD_DIM), BF16),
        in_specs=[sums] * 4
        + [weight] * 2
        + [pl.BlockSpec((each, per_head, per_device, HEAD_DIM), lambda h: (h, 0, 0, 0))]
        + ([] if first else [packed]),
        out_specs=packed,
        scratch_shapes=[pltpu.VMEM((RING * quarter, width), BF16)],
        compiler_params=params(24),
        cost_estimate=pl.CostEstimate(
            flops=4 * RING * quarter * width * columns,
            bytes_accessed=4 * width * columns,
            transcendentals=0,
        ),
    )(total, *received, key_weight, value_weight, queries, *([] if first else [before]))


def combine_kernel(at_ref, target_ref, packed_ref, own_ref, one_ref, two_ref, three_ref):
    target = target_ref[...]
    per_group = own_ref.shape[0]
    for shift, ref in enumerate((own_ref, one_ref, two_ref, three_ref)):
        group = lax.rem(at_ref[0] + shift, RING)
        match = target == iota((target.shape[0], per_group), 1) + group * per_group
        ref[...] = lax.dot_general(
            jnp.where(match, 1.0, 0.0).astype(BF16),
            packed_ref[...],
            (((0,), (0,)), ((), ())),
            preferred_element_type=F32,
        ).astype(ref.dtype)


def combine(at, target, packed, per_group):
    shape = (per_group, packed.shape[1])
    sent = jax.ShapeDtypeStruct(shape, BF16)
    return pl.pallas_call(
        combine_kernel,
        out_shape=(jax.ShapeDtypeStruct(shape, F32), sent, sent, sent),
        in_specs=[SMEM, VMEM, VMEM],
        out_specs=(VMEM,) * 4,
        compiler_params=params(16),
    )(at, target, packed)


def project_kernel(core, at_ref, own_ref, one_ref, two_ref, three_ref, weight_ref, out_ref):
    summed = own_ref[...]
    for ref in (one_ref, two_ref, three_ref):
        summed = summed + ref[...].astype(F32)
    divisor = summed[:, HEAD_DIM:]
    attended = summed[:, :HEAD_DIM] / jnp.where(divisor > 0.0, divisor, 1.0)
    half = attended.shape[0] // 2
    attended = jnp.concatenate([attended[:half], attended[half:]], axis=1).astype(BF16)
    here = at_ref[1]
    y_at, core_at = here // CORES % RING, here % CORES
    column = lax.rem(core_at + core, CORES)
    for y in range(RING):
        block = lax.rem(y_at + y, RING) * CORES + column
        at = pl.ds(pl.multiple_of(block * BLOCK, BLOCK), BLOCK)
        out_ref[0, y] = jnp.dot(
            attended, weight_ref[:, at], preferred_element_type=F32
        ).astype(BF16)


def project(at, own, received, weight, core):
    depth, columns = weight.shape
    rows = own.shape[0] // 2
    whole = pl.BlockSpec(own.shape, lambda z, at_ref: (0, 0))
    grid_spec = pltpu.PrefetchScalarGridSpec(
        num_scalar_prefetch=1,
        grid=(RING,),
        in_specs=[whole] * 4
        + [
            pl.BlockSpec(
                (depth, columns // RING),
                lambda z, at_ref: (0, lax.rem(at_ref[1] // (RING * CORES) + z, RING)),
            )
        ],
        out_specs=pl.BlockSpec((1, RING, rows, BLOCK), lambda z, at_ref: (z, 0, 0, 0)),
    )
    return pl.pallas_call(
        functools.partial(project_kernel, core),
        grid_spec=grid_spec,
        out_shape=jax.ShapeDtypeStruct((RING, RING, rows, BLOCK), BF16),
        compiler_params=params(16),
        cost_estimate=pl.CostEstimate(
            flops=rows * depth * columns, bytes_accessed=2 * depth * columns, transcendentals=0
        ),
    )(at, own, *received, weight)


def first_sum_kernel(kept_ref, got_ref, own_ref, one_ref, two_ref, three_ref):
    for shift, ref in enumerate((own_ref, one_ref, two_ref, three_ref)):
        ref[...] = (kept_ref[shift].astype(F32) + got_ref[shift].astype(F32)).astype(ref.dtype)


def first_sum(kept, got):
    sent = jax.ShapeDtypeStruct(kept.shape[1:], BF16)
    return pl.pallas_call(
        first_sum_kernel,
        out_shape=(jax.ShapeDtypeStruct(kept.shape[1:], F32), sent, sent, sent),
        in_specs=[VMEM, VMEM],
        out_specs=(VMEM,) * 4,
        compiler_params=params(16),
    )(kept, got)


def second_sum_kernel(kept_ref, a_ref, b_ref, c_ref, own_ref, one_ref, two_ref, three_ref):
    for shift, ref in enumerate((own_ref, one_ref, two_ref, three_ref)):
        summed = kept_ref[shift]
        for got in (a_ref, b_ref, c_ref):
            summed = summed + got[shift].astype(F32)
        ref[...] = summed.astype(ref.dtype)


def second_sum(kept, got):
    sent = jax.ShapeDtypeStruct(kept.shape[1:], BF16)
    return pl.pallas_call(
        second_sum_kernel,
        out_shape=(jax.ShapeDtypeStruct(kept.shape[1:], F32), sent, sent, sent),
        in_specs=[VMEM] * 4,
        out_specs=(VMEM,) * 4,
        compiler_params=params(16),
    )(kept, *got)


def last_sum_kernel(kept_ref, a_ref, b_ref, c_ref, residual_ref, out_ref):
    summed = kept_ref[...]
    for got in (a_ref, b_ref, c_ref):
        summed = summed + got[...].astype(F32)
    out_ref[...] = (residual_ref[...].astype(F32) + summed).astype(BF16)


def last_sum(kept, got, residual):
    return pl.pallas_call(
        last_sum_kernel,
        out_shape=jax.ShapeDtypeStruct(kept.shape, BF16),
        in_specs=[VMEM] * 5,
        out_specs=VMEM,
        compiler_params=params(16),
    )(kept, *got, residual)


def body(
    patches,
    enc_tiles,
    req_tiles,
    req_owner,
    fc1_weight,
    fc2_weight,
    key_weight,
    value_weight,
    query_weight,
    out_weight,
    text_hidden,
):
    capacity = patches.shape[0]
    devices = lax.axis_size("dev")
    local_heads = HEADS // devices
    slots, steps, model_width = text_hidden.shape
    dev_at = lax.axis_index("dev")
    at = jnp.stack([lax.axis_index("pool"), dev_at]).astype(jnp.int32)
    halves = capacity // RING

    own = [normalize(at, patches, i) for i in range(halves)]
    left = [pool_shift(own[i], 1) for i in range(halves)]
    right = [pool_shift(own[i], -1) for i in range(halves)]
    far_left = [pool_shift(left[i][: RING // 2], 1) for i in range(halves)]
    far_right = [pool_shift(right[i][RING // 2 :], -1) for i in range(halves)]

    text = text_hidden.reshape(slots * steps, model_width)
    query = make_query(text, query_weight)
    queries = [query] + [pool_shift(query, s) for s in range(1, RING)]
    chosen, target = select(
        at,
        enc_tiles.reshape(1, -1),
        req_tiles.reshape(1, -1),
        req_owner,
        queries,
        slots,
        steps,
        capacity,
    )
    per_device = halves * local_heads * steps
    tile_queries = lax.all_to_all(
        chosen.reshape(devices, per_device, HEAD_DIM), "dev", split_axis=0, concat_axis=0, tiled=True
    ).reshape(KV_HEADS, devices // KV_HEADS, per_device, HEAD_DIM)

    packed = None
    for i in range(halves):
        total, *messages = feed_forward(
            at, patches, own[i], left[i], right[i], far_left[i], far_right[i],
            fc1_weight, fc2_weight, i,
        )
        received = [pool_shift(messages[s - 1], s) for s in range(1, RING)]
        packed = attend(total, received, key_weight, value_weight, tile_queries, i, packed)
    packed = lax.all_to_all(
        packed.reshape(devices, per_device, 2 * HEAD_DIM),
        "dev",
        split_axis=0,
        concat_axis=0,
        tiled=True,
    ).reshape(devices * per_device, 2 * HEAD_DIM)
    summed, *messages = combine(at, target, packed, local_heads * slots * steps)
    received = [pool_shift(messages[s - 1], s) for s in range(1, RING)]

    away = dev_shift(project(at, summed, received, out_weight, 1), 0, 0, 1)
    kept = project(at, summed, received, out_weight, 0)
    kept, *messages = first_sum(kept, away)
    received = [dev_shift(messages[s - 1], s, 0, 0) for s in range(1, RING)]
    kept, *messages = second_sum(kept, received)
    received = [dev_shift(messages[s - 1], 0, s, 0) for s in range(1, RING)]
    width_out = model_width // devices
    residual = lax.dynamic_slice_in_dim(text, dev_at * width_out, width_out, 1)
    mixed = last_sum(kept, received, residual)
    return mixed.reshape(slots, steps, width_out)


def solution(mesh):
    return jax.shard_map(
        body,
        mesh=mesh,
        in_specs=(
            P("dev", "pool", None),
            P(),
            P(),
            P(),
            P(None, "pool"),
            P("pool", None),
            P(),
            P(),
            P(None, "dev"),
            P("dev", None),
            P("pool", None, None),
        ),
        out_specs=P("pool", None, "dev"),
        check_vma=False,
    )
```

```python
import functools

import jax
import jax.numpy as jnp
from jax import lax
from jax.experimental import pallas as pl
from jax.experimental.pallas import tpu as pltpu
from jax.sharding import PartitionSpec as P

HEADS = 64
KV_HEADS = 8
HEAD_DIM = 128
CORES = 2
RING = 4
BLOCK = 256
TOTAL_ROWS = 16
F32, BF16 = jnp.float32, jnp.bfloat16

epsilon = 1e-05

VMEM = pl.BlockSpec(memory_space=pltpu.VMEM)
SMEM = pl.BlockSpec(memory_space=pltpu.SMEM)


def params(mib):
    return pltpu.CompilerParams(vmem_limit_bytes=mib * 1024 * 1024)


def pool_shift(x, by):
    return lax.ppermute(x, "pool", [(i, (i + by) % RING) for i in range(RING)])


def dev_shift(x, by_z, by_y, by_core):
    pairs = []
    for z in range(RING):
        for y in range(RING):
            for k in range(CORES):
                to = ((z + by_z) % RING, (y + by_y) % RING, (k + by_core) % CORES)
                pairs.append(((z * RING + y) * CORES + k, (to[0] * RING + to[1]) * CORES + to[2]))
    return lax.ppermute(x, "dev", pairs)


def layer_rows(values):
    center = values - jnp.mean(values, axis=-1, keepdims=True)
    spread = jnp.mean(center * center, axis=-1, keepdims=True)
    return (center / jnp.sqrt(spread + epsilon)).astype(BF16)


def normalize_kernel(half, at_ref, patches_ref, rows_ref):
    for r in range(RING):
        slot = lax.rem(at_ref[0] + r, RING) + half * RING
        rows_ref[r] = layer_rows(patches_ref[slot].astype(F32))


def normalize(at, patches):
    _, quarter, width = patches.shape
    return pl.pallas_call(
        functools.partial(normalize_kernel, 0),
        out_shape=jax.ShapeDtypeStruct((RING, quarter, width), BF16),
        in_specs=[SMEM, VMEM],
        out_specs=VMEM,
        compiler_params=params(8),
    )(at, patches)


def hold_kernel(one_ref, two_ref, _, out_ref):
    out_ref[...] = jnp.zeros_like(out_ref)


def hold(one, two, after):
    return pl.pallas_call(
        hold_kernel,
        out_shape=jax.ShapeDtypeStruct((8, 128), F32),
        in_specs=[VMEM, VMEM, pl.BlockSpec(memory_space=pl.ANY)],
        out_specs=VMEM,
        compiler_params=params(8),
    )(one, two, after)


def feed_forward_kernel(
    half, at_ref, patches_ref, own_rows, one_rows, two_rows, three_rows, fc1_ref, fc2_ref, *refs
):
    total_ref, one_ref, two_ref, three_ref, rows_ref, wide_ref = refs[-6:]
    hidden, width = fc2_ref.shape
    quarter = patches_ref.shape[1]
    rows = RING * quarter
    for source, ref in enumerate((own_rows, one_rows, two_rows, three_rows)):
        rows_ref[source * rows : (source + 1) * rows] = ref[:RING].reshape(rows, width)
    for step in range(hidden // BLOCK):
        at = slice(step * BLOCK, (step + 1) * BLOCK)
        values = jnp.dot(rows_ref[...], fc1_ref[:, at], preferred_element_type=F32)
        wide_ref[:, at] = (0.5 * values * (1.0 + lax.erf(values * 0.5**0.5))).astype(BF16)
    outs = (total_ref, one_ref, two_ref, three_ref)
    for step in range(width // BLOCK):
        at = slice(step * BLOCK, (step + 1) * BLOCK)
        sums = jnp.dot(wide_ref[...], fc2_ref[:, at], preferred_element_type=F32)
        for source in range(RING):
            for m in range(RING):
                piece = sums[source * rows + m * quarter : source * rows + (m + 1) * quarter]
                shift = (m - source) % RING
                if source == 0:
                    slot = lax.rem(at_ref[0] + m, RING) + half * RING
                    piece = piece + patches_ref[slot, :, at].astype(F32)
                outs[shift][m, :, at] = piece.astype(outs[shift].dtype)


def feed_forward(at, patches, sources, fc1, fc2, half, after):
    _, quarter, width = patches.shape
    hidden = fc1.shape[1]
    shape = (RING, quarter, width)
    sent = jax.ShapeDtypeStruct(shape, BF16)
    return pl.pallas_call(
        functools.partial(feed_forward_kernel, half),
        out_shape=(sent,) * 4,
        in_specs=[SMEM] + [VMEM] * (7 + len(after)),
        out_specs=(VMEM,) * 4,
        scratch_shapes=[
            pltpu.VMEM((RING * RING * quarter, width), BF16),
            pltpu.VMEM((RING * RING * quarter, hidden), BF16),
        ],
        compiler_params=params(14),
        cost_estimate=pl.CostEstimate(
            flops=4 * RING * RING * quarter * width * hidden,
            bytes_accessed=4 * width * hidden,
            transcendentals=0,
        ),
    )(at, patches, *sources, fc1, fc2, *after)


def query_kernel(at_ref, text_ref, weight_ref, patches_ref, sent_ref, total_ref, square_ref):
    step = pl.program_id(0)
    rows, columns = total_ref.shape

    @pl.when(step == 0)
    def _():
        total_ref[...] = jnp.zeros_like(total_ref)
        square_ref[...] = jnp.zeros_like(square_ref)

    slot = lax.rem(at_ref[0] + step, RING) + RING
    sent_ref[step] = layer_rows(patches_ref[slot].astype(F32))
    text = text_ref[...].reshape(rows, text_ref.shape[-1])
    total_ref[...] += jnp.dot(text, weight_ref[...], preferred_element_type=F32)
    wide = text.astype(F32)
    square_ref[...] += jnp.sum(wide * wide, axis=-1, keepdims=True)

    @pl.when(step == pl.num_programs(0) - 1)
    def _():
        width = text_ref.shape[-1] * pl.num_programs(0)
        values = total_ref[...] / jnp.sqrt(square_ref[...] / width + epsilon)
        quarter = sent_ref.shape[1]
        for head in range(columns // HEAD_DIM):
            part = values[:, head * HEAD_DIM : (head + 1) * HEAD_DIM]
            mean = jnp.mean(part * part, axis=-1, keepdims=True)
            part = (part / jnp.sqrt(mean + epsilon)).astype(BF16)
            for piece in range(rows // quarter):
                lane = (head * (rows // quarter) + piece) * HEAD_DIM
                sent_ref[RING, :, lane : lane + HEAD_DIM] = part[
                    piece * quarter : (piece + 1) * quarter
                ]
        filled = columns // HEAD_DIM * (rows // quarter) * HEAD_DIM
        sent_ref[RING, :, filled:] = jnp.zeros((quarter, sent_ref.shape[2] - filled), BF16)


def second_half(at, text, weight, patches):
    slots, steps, model = text.shape
    rows = slots * steps
    _, quarter, width = patches.shape
    columns = weight.shape[1]
    depth = model // RING
    return pl.pallas_call(
        query_kernel,
        grid=(RING,),
        out_shape=jax.ShapeDtypeStruct((RING + 1, quarter, width), BF16),
        in_specs=[
            SMEM,
            pl.BlockSpec((slots, steps, depth), lambda k: (0, 0, k)),
            pl.BlockSpec((depth, columns), lambda k: (k, 0)),
            pl.BlockSpec(patches.shape, lambda k: (0, 0, 0)),
        ],
        out_specs=pl.BlockSpec((RING + 1, quarter, width), lambda k: (0, 0, 0)),
        scratch_shapes=[pltpu.VMEM((rows, columns), F32), pltpu.VMEM((rows, 1), F32)],
        compiler_params=params(12),
        cost_estimate=pl.CostEstimate(
            flops=2 * rows * model * columns,
            bytes_accessed=2 * model * (columns + rows),
            transcendentals=0,
        ),
    )(at, text, weight, patches)


def iota(shape, dim):
    return lax.broadcasted_iota(jnp.int32, shape, dim)


def select_kernel(
    slots, steps, heads, capacity, at_ref, enc_ref, req_ref, owner_ref,
    *refs,
):
    *sources, chosen_ref, target_ref = refs
    here = at_ref[0]
    columns, requests = enc_ref.shape[1], req_ref.shape[1]
    halves = capacity // RING
    per_group = heads * slots * steps
    rows = columns * halves * heads * steps
    before = iota((requests, requests), 0) < iota((requests, requests), 1)
    equal = iota((requests, requests), 0) == iota((requests, requests), 1)
    req_row = req_ref[...]
    req_column = jnp.sum(jnp.where(equal, req_row, 0), axis=1, keepdims=True)
    req_start = jnp.sum(jnp.where(before, req_column, 0), axis=0, keepdims=True)
    owner_column = owner_ref[...]
    owner_row = jnp.sum(jnp.where(equal, owner_column, 0), axis=0, keepdims=True)
    rank = jnp.sum(
        jnp.where(before & (owner_column == owner_row), 1, 0), axis=0, keepdims=True
    )
    place = owner_row * per_group + rank * steps
    enc_row = enc_ref[...]
    enc_equal = iota((columns, columns), 0) == iota((columns, columns), 1)
    enc_before = iota((columns, columns), 0) < iota((columns, columns), 1)
    enc_column = jnp.sum(jnp.where(enc_equal, enc_row, 0), axis=1, keepdims=True)
    enc_start = jnp.sum(jnp.where(enc_before, enc_column, 0), axis=0, keepdims=True)

    row = iota((rows, 1), 0)
    per_tile = heads * steps
    column = row // (halves * per_tile)
    slot = row // per_tile % halves * RING + here
    hit = column == iota((rows, columns), 1)
    count = jnp.sum(jnp.where(hit, enc_row, 0), axis=1, keepdims=True)
    start = jnp.sum(jnp.where(hit, enc_start, 0), axis=1, keepdims=True)
    tile = jnp.where(slot < count, start + slot, -1)
    has = (req_start <= tile) & (tile < req_start + req_row)
    base = jnp.sum(jnp.where(has, place + 1, 0), axis=1, keepdims=True) - 1
    within = row % per_tile
    target = jnp.where(base < 0, -1, base + within // steps * (slots * steps) + within % steps)
    target_ref[...] = target
    chosen = jnp.zeros((rows, HEAD_DIM), F32)
    for shift in range(RING):
        group = lax.rem(here - shift + RING, RING)
        ref = sources[0].at[group] if len(sources) == 1 else sources[shift]
        match = target == iota((rows, per_group), 1) + group * per_group
        chosen = chosen + jnp.dot(
            jnp.where(match, 1.0, 0.0).astype(BF16),
            jnp.concatenate(
                [
                    ref[RING, :, lane : lane + HEAD_DIM]
                    for lane in range(0, per_group // ref.shape[1] * HEAD_DIM, HEAD_DIM)
                ],
                axis=0,
            ),
            preferred_element_type=F32,
        )
    chosen_ref[...] = chosen.astype(BF16)


def select(at, enc, req, owner, queries, slots, steps, heads, capacity):
    rows = enc.shape[1] * (capacity // RING) * heads * steps
    return pl.pallas_call(
        functools.partial(select_kernel, slots, steps, heads, capacity),
        out_shape=(
            jax.ShapeDtypeStruct((rows, HEAD_DIM), BF16),
            jax.ShapeDtypeStruct((rows, 1), jnp.int32),
        ),
        in_specs=[SMEM] + [VMEM] * (3 + len(queries)),
        out_specs=(VMEM, VMEM),
        compiler_params=params(8),
    )(at, enc, req, owner, *queries)


def attend_kernel(half, total_ref, one_ref, two_ref, three_ref, key_ref, value_ref, query_ref, *refs):
    out_ref = refs[-1]
    _, quarter, width = total_ref.shape
    summed = total_ref[...].astype(F32)
    for ref in (one_ref, two_ref, three_ref):
        summed = summed + ref[...].astype(F32)
    vision = summed.astype(BF16).reshape(RING * quarter, width)
    heads, per_head, per_device, _ = query_ref.shape
    count = per_head * per_device
    mine = iota((count, 1), 0) % per_device // (per_device // 2) == half
    together = BLOCK // HEAD_DIM
    for pair in range(heads // together):
        at = slice(pair * BLOCK, (pair + 1) * BLOCK)
        keys = jnp.dot(vision, key_ref[:, at], preferred_element_type=F32)
        values = jnp.dot(vision, value_ref[:, at], preferred_element_type=F32).astype(BF16)
        for place in range(together):
            head = pair * together + place
            at = slice(place * HEAD_DIM, (place + 1) * HEAD_DIM)
            key = keys[:, at]
            mean = jnp.mean(key * key, axis=-1, keepdims=True)
            key = (key / jnp.sqrt(mean + epsilon)).astype(BF16)
            query = query_ref[head].reshape(count, HEAD_DIM)
            scores = lax.dot_general(
                query, key, (((1,), (1,)), ((), ())), preferred_element_type=F32
            ) * HEAD_DIM ** (-0.5)
            weights = jnp.where(mine, jnp.exp(scores), 0.0)
            divisor = jnp.sum(weights, axis=-1, keepdims=True)
            numerator = jnp.dot(weights.astype(BF16), values[:, at], preferred_element_type=F32)
            packed = jnp.concatenate(
                [numerator, jnp.broadcast_to(divisor, numerator.shape)], axis=1
            ).reshape(per_head, per_device, 2 * HEAD_DIM)
            if len(refs) > 1:
                packed = packed + refs[0][head].astype(F32)
            out_ref[head] = packed.astype(BF16)


def attend(total, received, key_weight, value_weight, queries, half, before):
    _, quarter, width = total.shape
    heads, per_head, per_device, _ = queries.shape
    columns = key_weight.shape[1]
    before = [] if before is None else [before]
    return pl.pallas_call(
        functools.partial(attend_kernel, half),
        out_shape=jax.ShapeDtypeStruct((heads, per_head, per_device, 2 * HEAD_DIM), BF16),
        in_specs=[VMEM] * (7 + len(before)),
        out_specs=VMEM,
        compiler_params=params(12),
        cost_estimate=pl.CostEstimate(
            flops=4 * RING * quarter * width * columns,
            bytes_accessed=4 * width * columns,
            transcendentals=0,
        ),
    )(total, *received, key_weight, value_weight, queries, *before)


def combine_kernel(at_ref, target_ref, packed_ref, own_ref, one_ref, two_ref, three_ref):
    target = target_ref[...]
    per_group = own_ref.shape[0] - TOTAL_ROWS
    for shift, ref in enumerate((own_ref, one_ref, two_ref, three_ref)):
        group = lax.rem(at_ref[0] + shift, RING)
        match = target == iota((target.shape[0], per_group), 1) + group * per_group
        summed = lax.dot_general(
            jnp.where(match, 1.0, 0.0).astype(BF16),
            packed_ref[...],
            (((0,), (0,)), ((), ())),
            preferred_element_type=F32,
        )
        ref[:per_group] = summed[:, :HEAD_DIM].astype(ref.dtype)
        totals = jnp.zeros((TOTAL_ROWS, HEAD_DIM), F32)
        for row, first in enumerate(range(0, per_group, HEAD_DIM)):
            part = summed[first : first + HEAD_DIM, HEAD_DIM:]
            lane = iota(part.shape, 0) == iota(part.shape, 1)
            part = jnp.sum(jnp.where(lane, part, 0.0), axis=0, keepdims=True)
            totals = jnp.where(iota(totals.shape, 0) == row, part, totals)
        ref[per_group:] = totals.astype(ref.dtype)


def combine(at, target, packed, per_group):
    shape = (per_group + TOTAL_ROWS, HEAD_DIM)
    sent = jax.ShapeDtypeStruct(shape, BF16)
    return pl.pallas_call(
        combine_kernel,
        out_shape=(jax.ShapeDtypeStruct(shape, F32), sent, sent, sent),
        in_specs=[SMEM, VMEM, VMEM],
        out_specs=(VMEM,) * 4,
        compiler_params=params(8),
    )(at, target, packed)


def project_kernel(core, at_ref, own_ref, one_ref, two_ref, three_ref, weight_ref, out_ref):
    summed = own_ref[...]
    for ref in (one_ref, two_ref, three_ref):
        summed = summed + ref[...].astype(F32)
    per_group = summed.shape[0] - TOTAL_ROWS
    attended = []
    for row, first in enumerate(range(0, per_group, HEAD_DIM)):
        part = summed[first : min(first + HEAD_DIM, per_group)]
        totals = jnp.broadcast_to(summed[per_group + row : per_group + row + 1], part.shape)
        lane = iota(part.shape, 0) == iota(part.shape, 1)
        divisor = jnp.sum(jnp.where(lane, totals, 0.0), axis=1, keepdims=True)
        attended.append(part / jnp.where(divisor > 0.0, divisor, 1.0))
    attended = jnp.concatenate(attended, axis=0)
    half = per_group // 2
    attended = jnp.concatenate([attended[:half], attended[half:]], axis=1).astype(BF16)
    here = at_ref[1]
    z_at, y_at, core_at = here // (RING * CORES), here // CORES % RING, here % CORES
    column = lax.rem(core_at + core, CORES)
    for z in range(RING):
        for y in range(RING):
            block = (
                lax.rem(z_at + z, RING) * RING + lax.rem(y_at + y, RING)
            ) * CORES + column
            at = pl.ds(pl.multiple_of(block * BLOCK, BLOCK), BLOCK)
            out_ref[z, y] = jnp.dot(
                attended, weight_ref[:, at], preferred_element_type=F32
            ).astype(BF16)


def project(at, own, received, weight, core):
    depth, columns = weight.shape
    rows = (own.shape[0] - TOTAL_ROWS) // 2
    return pl.pallas_call(
        functools.partial(project_kernel, core),
        out_shape=jax.ShapeDtypeStruct((RING, RING, rows, BLOCK), BF16),
        in_specs=[SMEM] + [VMEM] * 5,
        out_specs=VMEM,
        compiler_params=params(8),
        cost_estimate=pl.CostEstimate(
            flops=rows * depth * columns, bytes_accessed=2 * depth * columns, transcendentals=0
        ),
    )(at, own, *received, weight)


def first_sum_kernel(kept_ref, got_ref, own_ref, one_ref, two_ref, three_ref):
    for shift, ref in enumerate((own_ref, one_ref, two_ref, three_ref)):
        ref[...] = (kept_ref[shift].astype(F32) + got_ref[shift].astype(F32)).astype(ref.dtype)


def first_sum(kept, got):
    sent = jax.ShapeDtypeStruct(kept.shape[1:], BF16)
    return pl.pallas_call(
        first_sum_kernel,
        out_shape=(jax.ShapeDtypeStruct(kept.shape[1:], F32), sent, sent, sent),
        in_specs=[VMEM, VMEM],
        out_specs=(VMEM,) * 4,
        compiler_params=params(8),
    )(kept, got)


def second_sum_kernel(kept_ref, a_ref, b_ref, c_ref, own_ref, one_ref, two_ref, three_ref):
    for shift, ref in enumerate((own_ref, one_ref, two_ref, three_ref)):
        summed = kept_ref[shift]
        for got in (a_ref, b_ref, c_ref):
            summed = summed + got[shift].astype(F32)
        ref[...] = summed.astype(ref.dtype)


def second_sum(kept, got):
    sent = jax.ShapeDtypeStruct(kept.shape[1:], BF16)
    return pl.pallas_call(
        second_sum_kernel,
        out_shape=(jax.ShapeDtypeStruct(kept.shape[1:], F32), sent, sent, sent),
        in_specs=[VMEM] * 4,
        out_specs=(VMEM,) * 4,
        compiler_params=params(8),
    )(kept, *got)


def last_sum_kernel(kept_ref, a_ref, b_ref, c_ref, residual_ref, out_ref):
    summed = kept_ref[...]
    for got in (a_ref, b_ref, c_ref):
        summed = summed + got[...].astype(F32)
    out_ref[...] = (residual_ref[...].astype(F32) + summed.reshape(out_ref.shape)).astype(BF16)


def last_sum(kept, got, residual):
    return pl.pallas_call(
        last_sum_kernel,
        out_shape=jax.ShapeDtypeStruct(residual.shape, BF16),
        in_specs=[VMEM] * 5,
        out_specs=VMEM,
        compiler_params=params(8),
    )(kept, *got, residual)


def body(
    patches,
    enc_tiles,
    req_tiles,
    req_owner,
    fc1_weight,
    fc2_weight,
    key_weight,
    value_weight,
    query_weight,
    out_weight,
    text_hidden,
):
    capacity = patches.shape[0]
    devices = lax.axis_size("dev")
    local_heads = HEADS // devices
    slots, steps, model_width = text_hidden.shape
    dev_at = lax.axis_index("dev")
    at = jnp.stack([lax.axis_index("pool"), dev_at]).astype(jnp.int32)
    halves = capacity // RING

    own = [normalize(at, patches), second_half(at, text_hidden, query_weight, patches)]
    sources = [[rows] + [pool_shift(rows, s) for s in range(1, RING)] for rows in own]
    chosen, target = select(
        at,
        enc_tiles.reshape(1, -1),
        req_tiles.reshape(1, -1),
        req_owner,
        sources[1],
        slots,
        steps,
        local_heads,
        capacity,
    )
    per_device = halves * local_heads * steps
    tile_queries = lax.all_to_all(
        chosen.reshape(devices, per_device, HEAD_DIM), "dev", split_axis=0, concat_axis=0, tiled=True
    ).reshape(KV_HEADS, devices // KV_HEADS, per_device, HEAD_DIM)

    held = hold(fc1_weight, fc2_weight, sources[1][0])
    packed = None
    for i in range(halves):
        total, *messages = feed_forward(
            at, patches, sources[i], fc1_weight, fc2_weight, i,
            (held,),
        )
        received = [pool_shift(messages[s - 1], s) for s in range(1, RING)]
        packed = attend(total, received, key_weight, value_weight, tile_queries, i, packed)
    packed = lax.all_to_all(
        packed.reshape(devices, per_device, 2 * HEAD_DIM),
        "dev",
        split_axis=0,
        concat_axis=0,
        tiled=True,
    ).reshape(devices * per_device, 2 * HEAD_DIM)
    summed, *messages = combine(at, target, packed, local_heads * slots * steps)
    received = [pool_shift(messages[s - 1], s) for s in range(1, RING)]

    away = dev_shift(project(at, summed, received, out_weight, 1), 0, 0, 1)
    kept = project(at, summed, received, out_weight, 0)
    kept, *messages = first_sum(kept, away)
    received = [dev_shift(messages[s - 1], s, 0, 0) for s in range(1, RING)]
    kept, *messages = second_sum(kept, received)
    received = [dev_shift(messages[s - 1], 0, s, 0) for s in range(1, RING)]
    width_out = model_width // devices
    residual = lax.dynamic_slice_in_dim(text_hidden, dev_at * width_out, width_out, 2)
    return last_sum(kept, received, residual)


def solution(mesh):
    return jax.shard_map(
        body,
        mesh=mesh,
        in_specs=(
            P("dev", "pool", None),
            P(),
            P(),
            P(),
            P(None, "pool"),
            P("pool", None),
            P(),
            P(),
            P(None, "dev"),
            P("dev", None),
            P("pool", None, None),
        ),
        out_specs=P("pool", None, "dev"),
        check_vma=False,
    )
```

```python
import functools

import jax
import jax.numpy as jnp
from jax import lax
from jax.experimental import pallas as pl
from jax.experimental.pallas import tpu as pltpu
from jax.sharding import PartitionSpec as P

HEADS = 64
KV_HEADS = 8
HEAD_DIM = 128
CORES = 2
RING = 4
BLOCK = 256
TOTAL_ROWS = 16
ATTEND_MIB = 20
F32, BF16 = jnp.float32, jnp.bfloat16

epsilon = 1e-05

VMEM = pl.BlockSpec(memory_space=pltpu.VMEM)
SMEM = pl.BlockSpec(memory_space=pltpu.SMEM)


def params(mib):
    return pltpu.CompilerParams(vmem_limit_bytes=mib * 1024 * 1024)


def pool_shift(x, by):
    return lax.ppermute(x, "pool", [(i, (i + by) % RING) for i in range(RING)])


def dev_shift(x, by_z, by_y, by_core):
    pairs = []
    for z in range(RING):
        for y in range(RING):
            for k in range(CORES):
                to = ((z + by_z) % RING, (y + by_y) % RING, (k + by_core) % CORES)
                pairs.append(((z * RING + y) * CORES + k, (to[0] * RING + to[1]) * CORES + to[2]))
    return lax.ppermute(x, "dev", pairs)


def layer_rows(values):
    center = values - jnp.mean(values, axis=-1, keepdims=True)
    spread = jnp.mean(center * center, axis=-1, keepdims=True)
    return (center / jnp.sqrt(spread + epsilon)).astype(BF16)


def normalize_kernel(half, at_ref, patches_ref, rows_ref):
    for r in range(RING):
        slot = lax.rem(at_ref[0] + r, RING) + half * RING
        rows_ref[r] = layer_rows(patches_ref[slot].astype(F32))


def normalize(at, patches):
    _, quarter, width = patches.shape
    return pl.pallas_call(
        functools.partial(normalize_kernel, 0),
        out_shape=jax.ShapeDtypeStruct((RING, quarter, width), BF16),
        in_specs=[SMEM, VMEM],
        out_specs=VMEM,
        compiler_params=params(8),
    )(at, patches)


def hold_kernel(one_ref, two_ref, _, out_ref):
    out_ref[...] = jnp.zeros_like(out_ref)


def hold(one, two, after):
    return pl.pallas_call(
        hold_kernel,
        out_shape=jax.ShapeDtypeStruct((8, 128), F32),
        in_specs=[VMEM, VMEM, pl.BlockSpec(memory_space=pl.ANY)],
        out_specs=VMEM,
        compiler_params=params(8),
    )(one, two, after)


def feed_forward_kernel(
    half, at_ref, patches_ref, own_rows, one_rows, two_rows, three_rows, fc1_ref, fc2_ref, *refs
):
    total_ref, one_ref, two_ref, three_ref, *query_refs, rows_ref, wide_ref = refs[1:]
    for ref in query_refs:
        for source, rows in enumerate((own_rows, one_rows, two_rows, three_rows)):
            ref[source] = rows[RING]
    hidden, width = fc2_ref.shape
    quarter = patches_ref.shape[1]
    rows = RING * quarter
    for source, ref in enumerate((own_rows, one_rows, two_rows, three_rows)):
        rows_ref[source * rows : (source + 1) * rows] = ref[:RING].reshape(rows, width)
    for step in range(hidden // BLOCK):
        at = slice(step * BLOCK, (step + 1) * BLOCK)
        values = jnp.dot(rows_ref[...], fc1_ref[:, at], preferred_element_type=F32)
        wide_ref[:, at] = (0.5 * values * (1.0 + lax.erf(values * 0.5**0.5))).astype(BF16)
    outs = (total_ref, one_ref, two_ref, three_ref)
    for step in range(width // BLOCK):
        at = slice(step * BLOCK, (step + 1) * BLOCK)
        sums = jnp.dot(wide_ref[...], fc2_ref[:, at], preferred_element_type=F32)
        for source in range(RING):
            for m in range(RING):
                piece = sums[source * rows + m * quarter : source * rows + (m + 1) * quarter]
                shift = (m - source) % RING
                if source == 0:
                    slot = lax.rem(at_ref[0] + m, RING) + half * RING
                    piece = piece + patches_ref[slot, :, at].astype(F32)
                outs[shift][m, :, at] = piece.astype(outs[shift].dtype)


def feed_forward(at, patches, sources, fc1, fc2, half, after):
    _, quarter, width = patches.shape
    hidden = fc1.shape[1]
    shape = (RING, quarter, width)
    sent = jax.ShapeDtypeStruct(shape, BF16)
    return pl.pallas_call(
        functools.partial(feed_forward_kernel, half),
        out_shape=(sent,) * (4 + half),
        in_specs=[SMEM] + [VMEM] * (7 + len(after)),
        out_specs=(VMEM,) * (4 + half),
        scratch_shapes=[
            pltpu.VMEM((RING * RING * quarter, width), BF16),
            pltpu.VMEM((RING * RING * quarter, hidden), BF16),
        ],
        compiler_params=params(14),
        cost_estimate=pl.CostEstimate(
            flops=4 * RING * RING * quarter * width * hidden,
            bytes_accessed=4 * width * hidden,
            transcendentals=0,
        ),
    )(at, patches, *sources, fc1, fc2, *after)


def query_kernel(at_ref, text_ref, weight_ref, patches_ref, sent_ref, total_ref, square_ref):
    step = pl.program_id(0)
    rows, columns = total_ref.shape

    @pl.when(step == 0)
    def _():
        total_ref[...] = jnp.zeros_like(total_ref)
        square_ref[...] = jnp.zeros_like(square_ref)

    slot = lax.rem(at_ref[0] + step, RING) + RING
    sent_ref[step] = layer_rows(patches_ref[slot].astype(F32))
    text = text_ref[...].reshape(rows, text_ref.shape[-1])
    total_ref[...] += jnp.dot(text, weight_ref[...], preferred_element_type=F32)
    wide = text.astype(F32)
    square_ref[...] += jnp.sum(wide * wide, axis=-1, keepdims=True)

    @pl.when(step == pl.num_programs(0) - 1)
    def _():
        width = text_ref.shape[-1] * pl.num_programs(0)
        values = total_ref[...] / jnp.sqrt(square_ref[...] / width + epsilon)
        quarter = sent_ref.shape[1]
        for head in range(columns // HEAD_DIM):
            part = values[:, head * HEAD_DIM : (head + 1) * HEAD_DIM]
            mean = jnp.mean(part * part, axis=-1, keepdims=True)
            part = (part / jnp.sqrt(mean + epsilon)).astype(BF16)
            for piece in range(rows // quarter):
                lane = (head * (rows // quarter) + piece) * HEAD_DIM
                sent_ref[RING, :, lane : lane + HEAD_DIM] = part[
                    piece * quarter : (piece + 1) * quarter
                ]
        filled = columns // HEAD_DIM * (rows // quarter) * HEAD_DIM
        sent_ref[RING, :, filled:] = jnp.zeros((quarter, sent_ref.shape[2] - filled), BF16)


def second_half(at, text, weight, patches):
    slots, steps, model = text.shape
    rows = slots * steps
    _, quarter, width = patches.shape
    columns = weight.shape[1]
    depth = model // RING
    return pl.pallas_call(
        query_kernel,
        grid=(RING,),
        out_shape=jax.ShapeDtypeStruct((RING + 1, quarter, width), BF16),
        in_specs=[
            SMEM,
            pl.BlockSpec((slots, steps, depth), lambda k: (0, 0, k)),
            pl.BlockSpec((depth, columns), lambda k: (k, 0)),
            pl.BlockSpec(patches.shape, lambda k: (0, 0, 0)),
        ],
        out_specs=pl.BlockSpec((RING + 1, quarter, width), lambda k: (0, 0, 0)),
        scratch_shapes=[pltpu.VMEM((rows, columns), F32), pltpu.VMEM((rows, 1), F32)],
        compiler_params=params(12),
        cost_estimate=pl.CostEstimate(
            flops=2 * rows * model * columns,
            bytes_accessed=2 * model * (columns + rows),
            transcendentals=0,
        ),
    )(at, text, weight, patches)


def iota(shape, dim):
    return lax.broadcasted_iota(jnp.int32, shape, dim)


def select_kernel(
    slots, steps, heads, capacity, at_ref, enc_ref, req_ref, owner_ref,
    *refs,
):
    sources, chosen_ref, target_ref = refs
    here = at_ref[0]
    columns, requests = enc_ref.shape[1], req_ref.shape[1]
    halves = capacity // RING
    per_group = heads * slots * steps
    rows = columns * halves * heads * steps
    before = iota((requests, requests), 0) < iota((requests, requests), 1)
    equal = iota((requests, requests), 0) == iota((requests, requests), 1)
    req_row = req_ref[...]
    req_column = jnp.sum(jnp.where(equal, req_row, 0), axis=1, keepdims=True)
    req_start = jnp.sum(jnp.where(before, req_column, 0), axis=0, keepdims=True)
    owner_column = owner_ref[...]
    owner_row = jnp.sum(jnp.where(equal, owner_column, 0), axis=0, keepdims=True)
    rank = jnp.sum(
        jnp.where(before & (owner_column == owner_row), 1, 0), axis=0, keepdims=True
    )
    place = owner_row * per_group + rank * steps
    enc_row = enc_ref[...]
    enc_equal = iota((columns, columns), 0) == iota((columns, columns), 1)
    enc_before = iota((columns, columns), 0) < iota((columns, columns), 1)
    enc_column = jnp.sum(jnp.where(enc_equal, enc_row, 0), axis=1, keepdims=True)
    enc_start = jnp.sum(jnp.where(enc_before, enc_column, 0), axis=0, keepdims=True)

    row = iota((rows, 1), 0)
    per_tile = heads * steps
    column = row // (halves * per_tile)
    slot = row // per_tile % halves * RING + here
    hit = column == iota((rows, columns), 1)
    count = jnp.sum(jnp.where(hit, enc_row, 0), axis=1, keepdims=True)
    start = jnp.sum(jnp.where(hit, enc_start, 0), axis=1, keepdims=True)
    tile = jnp.where(slot < count, start + slot, -1)
    has = (req_start <= tile) & (tile < req_start + req_row)
    base = jnp.sum(jnp.where(has, place + 1, 0), axis=1, keepdims=True) - 1
    within = row % per_tile
    target = jnp.where(base < 0, -1, base + within // steps * (slots * steps) + within % steps)
    target_ref[...] = target
    chosen = jnp.zeros((rows, HEAD_DIM), F32)
    for shift in range(RING):
        group = lax.rem(here - shift + RING, RING)
        match = target == iota((rows, per_group), 1) + group * per_group
        chosen = chosen + jnp.dot(
            jnp.where(match, 1.0, 0.0).astype(BF16),
            jnp.concatenate(
                [
                    sources[shift, :, lane : lane + HEAD_DIM]
                    for lane in range(0, per_group // sources.shape[1] * HEAD_DIM, HEAD_DIM)
                ],
                axis=0,
            ),
            preferred_element_type=F32,
        )
    chosen_ref[...] = chosen.astype(BF16)


def select(at, enc, req, owner, queries, slots, steps, heads, capacity):
    rows = enc.shape[1] * (capacity // RING) * heads * steps
    return pl.pallas_call(
        functools.partial(select_kernel, slots, steps, heads, capacity),
        out_shape=(
            jax.ShapeDtypeStruct((rows, HEAD_DIM), BF16),
            jax.ShapeDtypeStruct((rows, 1), jnp.int32),
        ),
        in_specs=[SMEM] + [VMEM] * 4,
        out_specs=(VMEM, VMEM),
        compiler_params=params(8),
    )(at, enc, req, owner, queries)


def attend_kernel(*refs):
    count = 2 * RING
    sums, (key_hbm, value_hbm, query_hbm) = refs[:count], refs[count : count + 3]
    out_ref, sums_ref, rows_ref, key_ref, value_ref, query_ref, sum_sems, weight_sems = refs[count + 3 :]
    _, ring, quarter, width = sums_ref.shape
    heads, per_head, per_device, _ = query_ref.shape
    pairs = heads * HEAD_DIM // BLOCK
    copies = [
        pltpu.make_async_copy(ref, sums_ref.at[i], sum_sems.at[i]) for i, ref in enumerate(sums)
    ]
    copies.append(pltpu.make_async_copy(query_hbm, query_ref, sum_sems.at[count]))
    weight_copies = []
    for pair in range(pairs):
        at = pl.ds(pair * BLOCK, BLOCK)
        weight_copies.append(
            [
                pltpu.make_async_copy(hbm.at[:, at], ref.at[:, at], weight_sems.at[i, pair])
                for i, (hbm, ref) in enumerate(((key_hbm, key_ref), (value_hbm, value_ref)))
            ]
        )
    for copy in copies + weight_copies[0]:
        copy.start()
    for more in weight_copies[1:]:
        for copy in more:
            copy.start()
    rows = ring * quarter
    for half in range(2):
        for i in range(half * RING, (half + 1) * RING):
            copies[i].wait()
        summed = sums_ref[half * RING].astype(F32)
        for i in range(half * RING + 1, (half + 1) * RING):
            summed = summed + sums_ref[i].astype(F32)
        rows_ref[half * rows : (half + 1) * rows] = summed.astype(BF16).reshape(rows, width)
    copies[count].wait()
    many = per_head * per_device
    mine = (
        iota((many, 2 * rows), 0) % per_device // (per_device // 2)
        == iota((many, 2 * rows), 1) // rows
    )
    together = BLOCK // HEAD_DIM
    for pair in range(pairs):
        at = slice(pair * BLOCK, (pair + 1) * BLOCK)
        for copy in weight_copies[pair]:
            copy.wait()
        keys = jnp.dot(rows_ref[...], key_ref[:, at], preferred_element_type=F32)
        values = jnp.dot(rows_ref[...], value_ref[:, at], preferred_element_type=F32).astype(BF16)
        for place in range(together):
            head = pair * together + place
            at = slice(place * HEAD_DIM, (place + 1) * HEAD_DIM)
            key = keys[:, at]
            mean = jnp.mean(key * key, axis=-1, keepdims=True)
            key = (key / jnp.sqrt(mean + epsilon)).astype(BF16)
            query = query_ref[head].reshape(many, HEAD_DIM)
            scores = lax.dot_general(
                query, key, (((1,), (1,)), ((), ())), preferred_element_type=F32
            ) * HEAD_DIM ** (-0.5)
            weights = jnp.where(mine, jnp.exp(scores), 0.0)
            divisor = jnp.sum(weights, axis=-1, keepdims=True)
            numerator = jnp.dot(weights.astype(BF16), values[:, at], preferred_element_type=F32)
            out_ref[head] = (
                jnp.concatenate(
                    [numerator, jnp.broadcast_to(divisor, numerator.shape)], axis=1
                )
                .reshape(per_head, per_device, 2 * HEAD_DIM)
                .astype(BF16)
            )


def attend(sums, key_weight, value_weight, queries):
    shape = sums[0].shape
    _, quarter, width = shape
    heads, per_head, per_device, _ = queries.shape
    columns = key_weight.shape[1]
    return pl.pallas_call(
        attend_kernel,
        out_shape=jax.ShapeDtypeStruct((heads, per_head, per_device, 2 * HEAD_DIM), BF16),
        in_specs=[pl.BlockSpec(memory_space=pl.ANY)] * (len(sums) + 3),
        out_specs=VMEM,
        scratch_shapes=[
            pltpu.VMEM((len(sums),) + shape, BF16),
            pltpu.VMEM((2 * RING * quarter, width), BF16),
            pltpu.VMEM(key_weight.shape, BF16),
            pltpu.VMEM(value_weight.shape, BF16),
            pltpu.VMEM(queries.shape, BF16),
            pltpu.SemaphoreType.DMA((len(sums) + 1,)),
            pltpu.SemaphoreType.DMA((2, columns // BLOCK)),
        ],
        compiler_params=params(ATTEND_MIB),
        cost_estimate=pl.CostEstimate(
            flops=8 * RING * quarter * width * columns,
            bytes_accessed=4 * width * columns,
            transcendentals=0,
        ),
    )(*sums, key_weight, value_weight, queries)


def combine_kernel(at_ref, target_ref, packed_ref, own_ref, one_ref, two_ref, three_ref):
    target = target_ref[...]
    per_group = own_ref.shape[0] - TOTAL_ROWS
    for shift, ref in enumerate((own_ref, one_ref, two_ref, three_ref)):
        group = lax.rem(at_ref[0] + shift, RING)
        match = target == iota((target.shape[0], per_group), 1) + group * per_group
        summed = lax.dot_general(
            jnp.where(match, 1.0, 0.0).astype(BF16),
            packed_ref[...],
            (((0,), (0,)), ((), ())),
            preferred_element_type=F32,
        )
        ref[:per_group] = summed[:, :HEAD_DIM].astype(ref.dtype)
        totals = jnp.zeros((TOTAL_ROWS, HEAD_DIM), F32)
        for row, first in enumerate(range(0, per_group, HEAD_DIM)):
            part = summed[first : first + HEAD_DIM, HEAD_DIM:]
            lane = iota(part.shape, 0) == iota(part.shape, 1)
            part = jnp.sum(jnp.where(lane, part, 0.0), axis=0, keepdims=True)
            totals = jnp.where(iota(totals.shape, 0) == row, part, totals)
        ref[per_group:] = totals.astype(ref.dtype)


def combine(at, target, packed, per_group):
    shape = (per_group + TOTAL_ROWS, HEAD_DIM)
    sent = jax.ShapeDtypeStruct(shape, BF16)
    return pl.pallas_call(
        combine_kernel,
        out_shape=(jax.ShapeDtypeStruct(shape, F32), sent, sent, sent),
        in_specs=[SMEM, VMEM, VMEM],
        out_specs=(VMEM,) * 4,
        compiler_params=params(8),
    )(at, target, packed)


def project_kernel(core, at_ref, own_ref, one_ref, two_ref, three_ref, weight_ref, out_ref):
    summed = own_ref[...]
    for ref in (one_ref, two_ref, three_ref):
        summed = summed + ref[...].astype(F32)
    per_group = summed.shape[0] - TOTAL_ROWS
    attended = []
    for row, first in enumerate(range(0, per_group, HEAD_DIM)):
        part = summed[first : min(first + HEAD_DIM, per_group)]
        totals = jnp.broadcast_to(summed[per_group + row : per_group + row + 1], part.shape)
        lane = iota(part.shape, 0) == iota(part.shape, 1)
        divisor = jnp.sum(jnp.where(lane, totals, 0.0), axis=1, keepdims=True)
        attended.append(part / jnp.where(divisor > 0.0, divisor, 1.0))
    attended = jnp.concatenate(attended, axis=0)
    half = per_group // 2
    attended = jnp.concatenate([attended[:half], attended[half:]], axis=1).astype(BF16)
    here = at_ref[1]
    z_at, y_at, core_at = here // (RING * CORES), here // CORES % RING, here % CORES
    column = lax.rem(core_at + core, CORES)
    for z in range(RING):
        for y in range(RING):
            block = (
                lax.rem(z_at + z, RING) * RING + lax.rem(y_at + y, RING)
            ) * CORES + column
            at = pl.ds(pl.multiple_of(block * BLOCK, BLOCK), BLOCK)
            out_ref[z, y] = jnp.dot(
                attended, weight_ref[:, at], preferred_element_type=F32
            ).astype(BF16)


def project(at, own, received, weight, core):
    depth, columns = weight.shape
    rows = (own.shape[0] - TOTAL_ROWS) // 2
    return pl.pallas_call(
        functools.partial(project_kernel, core),
        out_shape=jax.ShapeDtypeStruct((RING, RING, rows, BLOCK), BF16),
        in_specs=[SMEM] + [VMEM] * 5,
        out_specs=VMEM,
        compiler_params=params(8),
        cost_estimate=pl.CostEstimate(
            flops=rows * depth * columns, bytes_accessed=2 * depth * columns, transcendentals=0
        ),
    )(at, own, *received, weight)


def first_sum_kernel(kept_ref, got_ref, own_ref, one_ref, two_ref, three_ref):
    for shift, ref in enumerate((own_ref, one_ref, two_ref, three_ref)):
        ref[...] = (kept_ref[shift].astype(F32) + got_ref[shift].astype(F32)).astype(ref.dtype)


def first_sum(kept, got):
    sent = jax.ShapeDtypeStruct(kept.shape[1:], BF16)
    return pl.pallas_call(
        first_sum_kernel,
        out_shape=(jax.ShapeDtypeStruct(kept.shape[1:], F32), sent, sent, sent),
        in_specs=[VMEM, VMEM],
        out_specs=(VMEM,) * 4,
        compiler_params=params(8),
    )(kept, got)


def second_sum_kernel(kept_ref, a_ref, b_ref, c_ref, own_ref, one_ref, two_ref, three_ref):
    for shift, ref in enumerate((own_ref, one_ref, two_ref, three_ref)):
        summed = kept_ref[shift]
        for got in (a_ref, b_ref, c_ref):
            summed = summed + got[shift].astype(F32)
        ref[...] = summed.astype(ref.dtype)


def second_sum(kept, got):
    sent = jax.ShapeDtypeStruct(kept.shape[1:], BF16)
    return pl.pallas_call(
        second_sum_kernel,
        out_shape=(jax.ShapeDtypeStruct(kept.shape[1:], F32), sent, sent, sent),
        in_specs=[VMEM] * 4,
        out_specs=(VMEM,) * 4,
        compiler_params=params(8),
    )(kept, *got)


def last_sum_kernel(kept_ref, a_ref, b_ref, c_ref, residual_ref, out_ref):
    summed = kept_ref[...]
    for got in (a_ref, b_ref, c_ref):
        summed = summed + got[...].astype(F32)
    out_ref[...] = (residual_ref[...].astype(F32) + summed.reshape(out_ref.shape)).astype(BF16)


def last_sum(kept, got, residual):
    return pl.pallas_call(
        last_sum_kernel,
        out_shape=jax.ShapeDtypeStruct(residual.shape, BF16),
        in_specs=[VMEM] * 5,
        out_specs=VMEM,
        compiler_params=params(8),
    )(kept, *got, residual)


def body(
    patches,
    enc_tiles,
    req_tiles,
    req_owner,
    fc1_weight,
    fc2_weight,
    key_weight,
    value_weight,
    query_weight,
    out_weight,
    text_hidden,
):
    capacity = patches.shape[0]
    devices = lax.axis_size("dev")
    local_heads = HEADS // devices
    slots, steps, model_width = text_hidden.shape
    dev_at = lax.axis_index("dev")
    at = jnp.stack([lax.axis_index("pool"), dev_at]).astype(jnp.int32)
    halves = capacity // RING

    own = [normalize(at, patches), second_half(at, text_hidden, query_weight, patches)]
    sources = [[rows] + [pool_shift(rows, s) for s in range(1, RING)] for rows in own]
    held = hold(fc1_weight, fc2_weight, sources[1][0])
    sums, queries = [], None
    for i in range(halves):
        total, *messages = feed_forward(
            at, patches, sources[i], fc1_weight, fc2_weight, i, (held,)
        )
        queries = messages[-1]
        sums += [total] + [pool_shift(messages[s - 1], s) for s in range(1, RING)]
    chosen, target = select(
        at,
        enc_tiles.reshape(1, -1),
        req_tiles.reshape(1, -1),
        req_owner,
        queries,
        slots,
        steps,
        local_heads,
        capacity,
    )
    per_device = halves * local_heads * steps
    tile_queries = lax.all_to_all(
        chosen.reshape(devices, per_device, HEAD_DIM), "dev", split_axis=0, concat_axis=0, tiled=True
    ).reshape(KV_HEADS, devices // KV_HEADS, per_device, HEAD_DIM)
    packed = attend(sums, key_weight, value_weight, tile_queries)
    packed = lax.all_to_all(
        packed.reshape(devices, per_device, 2 * HEAD_DIM),
        "dev",
        split_axis=0,
        concat_axis=0,
        tiled=True,
    ).reshape(devices * per_device, 2 * HEAD_DIM)
    summed, *messages = combine(at, target, packed, local_heads * slots * steps)
    received = [pool_shift(messages[s - 1], s) for s in range(1, RING)]

    away = dev_shift(project(at, summed, received, out_weight, 1), 0, 0, 1)
    kept = project(at, summed, received, out_weight, 0)
    kept, *messages = first_sum(kept, away)
    received = [dev_shift(messages[s - 1], s, 0, 0) for s in range(1, RING)]
    kept, *messages = second_sum(kept, received)
    received = [dev_shift(messages[s - 1], 0, s, 0) for s in range(1, RING)]
    width_out = model_width // devices
    residual = lax.dynamic_slice_in_dim(text_hidden, dev_at * width_out, width_out, 2)
    return last_sum(kept, received, residual)


def solution(mesh):
    return jax.shard_map(
        body,
        mesh=mesh,
        in_specs=(
            P("dev", "pool", None),
            P(),
            P(),
            P(),
            P(None, "pool"),
            P("pool", None),
            P(),
            P(),
            P(None, "dev"),
            P("dev", None),
            P("pool", None, None),
        ),
        out_specs=P("pool", None, "dev"),
        check_vma=False,
    )
```

```python
import functools

import jax
import jax.numpy as jnp
from jax import lax
from jax.experimental import pallas as pl
from jax.experimental.pallas import tpu as pltpu
from jax.sharding import PartitionSpec as P

HEADS = 64
KV_HEADS = 8
HEAD_DIM = 128
CORES = 2
RING = 4
BLOCK = 256
TOTAL_ROWS = 16
ATTEND_MIB = 20
F32, BF16 = jnp.float32, jnp.bfloat16

epsilon = 1e-05

VMEM = pl.BlockSpec(memory_space=pltpu.VMEM)
SMEM = pl.BlockSpec(memory_space=pltpu.SMEM)


def params(mib):
    return pltpu.CompilerParams(vmem_limit_bytes=mib * 1024 * 1024)


def pool_shift(x, by):
    return lax.ppermute(x, "pool", [(i, (i + by) % RING) for i in range(RING)])


def dev_shift(x, by_z, by_y, by_core):
    pairs = []
    for z in range(RING):
        for y in range(RING):
            for k in range(CORES):
                to = ((z + by_z) % RING, (y + by_y) % RING, (k + by_core) % CORES)
                pairs.append(((z * RING + y) * CORES + k, (to[0] * RING + to[1]) * CORES + to[2]))
    return lax.ppermute(x, "dev", pairs)


def layer_rows(values):
    center = values - jnp.mean(values, axis=-1, keepdims=True)
    spread = jnp.mean(center * center, axis=-1, keepdims=True)
    return (center / jnp.sqrt(spread + epsilon)).astype(BF16)


def normalize_kernel(half, at_ref, patches_ref, rows_ref):
    for r in range(RING):
        slot = lax.rem(at_ref[0] + r, RING) + half * RING
        rows_ref[r] = layer_rows(patches_ref[slot].astype(F32))


def normalize(at, patches):
    _, quarter, width = patches.shape
    return pl.pallas_call(
        functools.partial(normalize_kernel, 0),
        out_shape=jax.ShapeDtypeStruct((RING, quarter, width), BF16),
        in_specs=[SMEM, VMEM],
        out_specs=VMEM,
        compiler_params=params(8),
    )(at, patches)


def hold_kernel(one_ref, two_ref, _, out_ref):
    out_ref[...] = jnp.zeros_like(out_ref)


def hold(one, two, after):
    return pl.pallas_call(
        hold_kernel,
        out_shape=jax.ShapeDtypeStruct((8, 128), F32),
        in_specs=[VMEM, VMEM, pl.BlockSpec(memory_space=pl.ANY)],
        out_specs=VMEM,
        compiler_params=params(8),
    )(one, two, after)


def feed_forward_kernel(
    half, at_ref, patches_ref, own_rows, one_rows, two_rows, three_rows, fc1_ref, fc2_ref, *refs
):
    total_ref, one_ref, two_ref, three_ref, *query_refs, rows_ref, wide_ref = refs[2:]
    for ref in query_refs:
        for source, rows in enumerate((own_rows, one_rows, two_rows, three_rows)):
            ref[source] = rows[RING]
    hidden, width = fc2_ref.shape
    quarter = patches_ref.shape[1]
    rows = RING * quarter
    for source, ref in enumerate((own_rows, one_rows, two_rows, three_rows)):
        rows_ref[source * rows : (source + 1) * rows] = ref[:RING].reshape(rows, width)
    for step in range(hidden // BLOCK):
        at = slice(step * BLOCK, (step + 1) * BLOCK)
        values = jnp.dot(rows_ref[...], fc1_ref[:, at], preferred_element_type=F32)
        wide_ref[:, at] = (0.5 * values * (1.0 + lax.erf(values * 0.5**0.5))).astype(BF16)
    outs = (total_ref, one_ref, two_ref, three_ref)
    for step in range(width // BLOCK):
        at = slice(step * BLOCK, (step + 1) * BLOCK)
        sums = jnp.dot(wide_ref[...], fc2_ref[:, at], preferred_element_type=F32)
        for source in range(RING):
            for m in range(RING):
                piece = sums[source * rows + m * quarter : source * rows + (m + 1) * quarter]
                shift = (m - source) % RING
                if source == 0:
                    slot = lax.rem(at_ref[0] + m, RING) + half * RING
                    piece = piece + patches_ref[slot, :, at].astype(F32)
                outs[shift][m, :, at] = piece.astype(outs[shift].dtype)


def feed_forward(at, patches, sources, fc1, fc2, half, after):
    _, quarter, width = patches.shape
    hidden = fc1.shape[1]
    shape = (RING, quarter, width)
    sent = jax.ShapeDtypeStruct(shape, BF16)
    return pl.pallas_call(
        functools.partial(feed_forward_kernel, half),
        out_shape=(sent,) * (4 + half),
        in_specs=[SMEM] + [VMEM] * (7 + len(after)),
        out_specs=(VMEM,) * (4 + half),
        scratch_shapes=[
            pltpu.VMEM((RING * RING * quarter, width), BF16),
            pltpu.VMEM((RING * RING * quarter, hidden), BF16),
        ],
        compiler_params=params(14),
        cost_estimate=pl.CostEstimate(
            flops=4 * RING * RING * quarter * width * hidden,
            bytes_accessed=4 * width * hidden,
            transcendentals=0,
        ),
    )(at, patches, *sources, fc1, fc2, *after)


def query_kernel(at_ref, text_ref, weight_ref, patches_ref, sent_ref, total_ref, square_ref):
    step = pl.program_id(0)
    rows, columns = total_ref.shape

    @pl.when(step == 0)
    def _():
        total_ref[...] = jnp.zeros_like(total_ref)
        square_ref[...] = jnp.zeros_like(square_ref)

    slot = lax.rem(at_ref[0] + step, RING) + RING
    sent_ref[step] = layer_rows(patches_ref[slot].astype(F32))
    text = text_ref[...].reshape(rows, text_ref.shape[-1])
    total_ref[...] += jnp.dot(text, weight_ref[...], preferred_element_type=F32)
    wide = text.astype(F32)
    square_ref[...] += jnp.sum(wide * wide, axis=-1, keepdims=True)

    @pl.when(step == pl.num_programs(0) - 1)
    def _():
        width = text_ref.shape[-1] * pl.num_programs(0)
        values = total_ref[...] / jnp.sqrt(square_ref[...] / width + epsilon)
        quarter = sent_ref.shape[1]
        for head in range(columns // HEAD_DIM):
            part = values[:, head * HEAD_DIM : (head + 1) * HEAD_DIM]
            mean = jnp.mean(part * part, axis=-1, keepdims=True)
            part = (part / jnp.sqrt(mean + epsilon)).astype(BF16)
            for piece in range(rows // quarter):
                lane = (head * (rows // quarter) + piece) * HEAD_DIM
                sent_ref[RING, :, lane : lane + HEAD_DIM] = part[
                    piece * quarter : (piece + 1) * quarter
                ]
        filled = columns // HEAD_DIM * (rows // quarter) * HEAD_DIM
        sent_ref[RING, :, filled:] = jnp.zeros((quarter, sent_ref.shape[2] - filled), BF16)


def second_half(at, text, weight, patches):
    slots, steps, model = text.shape
    rows = slots * steps
    _, quarter, width = patches.shape
    columns = weight.shape[1]
    depth = model // RING
    return pl.pallas_call(
        query_kernel,
        grid=(RING,),
        out_shape=jax.ShapeDtypeStruct((RING + 1, quarter, width), BF16),
        in_specs=[
            SMEM,
            pl.BlockSpec((slots, steps, depth), lambda k: (0, 0, k)),
            pl.BlockSpec((depth, columns), lambda k: (k, 0)),
            pl.BlockSpec(patches.shape, lambda k: (0, 0, 0)),
        ],
        out_specs=pl.BlockSpec((RING + 1, quarter, width), lambda k: (0, 0, 0)),
        scratch_shapes=[pltpu.VMEM((rows, columns), F32), pltpu.VMEM((rows, 1), F32)],
        compiler_params=params(12),
        cost_estimate=pl.CostEstimate(
            flops=2 * rows * model * columns,
            bytes_accessed=2 * model * (columns + rows),
            transcendentals=0,
        ),
    )(at, text, weight, patches)


def iota(shape, dim):
    return lax.broadcasted_iota(jnp.int32, shape, dim)


def tables_kernel(
    slots, steps, heads, capacity, at_ref, enc_ref, req_ref, owner_ref, _, target_ref
):
    columns, requests = enc_ref.shape[1], req_ref.shape[1]
    halves = capacity // RING
    per_group = heads * slots * steps
    rows = target_ref.shape[0]
    before = iota((requests, requests), 0) < iota((requests, requests), 1)
    equal = iota((requests, requests), 0) == iota((requests, requests), 1)
    req_row = req_ref[...]
    req_column = jnp.sum(jnp.where(equal, req_row, 0), axis=1, keepdims=True)
    req_start = jnp.sum(jnp.where(before, req_column, 0), axis=0, keepdims=True)
    owner_column = owner_ref[...]
    owner_row = jnp.sum(jnp.where(equal, owner_column, 0), axis=0, keepdims=True)
    rank = jnp.sum(
        jnp.where(before & (owner_column == owner_row), 1, 0), axis=0, keepdims=True
    )
    place = owner_row * per_group + rank * steps
    enc_row = enc_ref[...]
    enc_equal = iota((columns, columns), 0) == iota((columns, columns), 1)
    enc_before = iota((columns, columns), 0) < iota((columns, columns), 1)
    enc_column = jnp.sum(jnp.where(enc_equal, enc_row, 0), axis=1, keepdims=True)
    enc_start = jnp.sum(jnp.where(enc_before, enc_column, 0), axis=0, keepdims=True)

    row = iota((rows, 1), 0)
    per_tile = heads * steps
    column = row // (halves * per_tile)
    slot = row // per_tile % halves * RING + at_ref[0]
    within = row % per_tile
    hit = column == iota((rows, columns), 1)
    count = jnp.sum(jnp.where(hit, enc_row, 0), axis=1, keepdims=True)
    start = jnp.sum(jnp.where(hit, enc_start, 0), axis=1, keepdims=True)
    tile = jnp.where(slot < count, start + slot, -1)
    has = (req_start <= tile) & (tile < req_start + req_row)
    base = jnp.sum(jnp.where(has, place + 1, 0), axis=1, keepdims=True) - 1
    target_ref[...] = jnp.where(
        base < 0, -1, base + within // steps * (slots * steps) + within % steps
    )


def tables(at, enc, req, owner, slots, steps, heads, capacity, after):
    rows = enc.shape[1] * (capacity // RING) * heads * steps
    return pl.pallas_call(
        functools.partial(tables_kernel, slots, steps, heads, capacity),
        out_shape=jax.ShapeDtypeStruct((rows, 1), jnp.int32),
        in_specs=[SMEM] + [VMEM] * 3 + [pl.BlockSpec(memory_space=pl.ANY)],
        out_specs=VMEM,
        compiler_params=params(8),
    )(at, enc, req, owner, after)


def select_kernel(per_group, at_ref, target_ref, sources_ref, chosen_ref):
    target = target_ref[...]
    chosen = jnp.zeros(chosen_ref.shape, F32)
    for shift in range(RING):
        group = lax.rem(at_ref[0] - shift + RING, RING)
        match = target == iota((target.shape[0], per_group), 1) + group * per_group
        pieces = per_group // sources_ref.shape[1]
        queries = jnp.concatenate(
            [
                sources_ref[shift, :, i * HEAD_DIM : (i + 1) * HEAD_DIM]
                for i in range(pieces)
            ],
            axis=0,
        )
        chosen = chosen + jnp.dot(
            jnp.where(match, 1.0, 0.0).astype(BF16), queries, preferred_element_type=F32
        )
    chosen_ref[...] = chosen.astype(BF16)


def select(at, target, sources, per_group):
    return pl.pallas_call(
        functools.partial(select_kernel, per_group),
        out_shape=jax.ShapeDtypeStruct((target.shape[0], HEAD_DIM), BF16),
        in_specs=[SMEM, VMEM, VMEM],
        out_specs=VMEM,
        compiler_params=params(8),
    )(at, target, sources)


def attend_kernel(*refs):
    count = 2 * RING
    sums, (key_hbm, value_hbm, query_hbm) = refs[:count], refs[count : count + 3]
    out_ref, sums_ref, rows_ref, key_ref, value_ref, query_ref, sum_sems, weight_sems = refs[count + 3 :]
    _, ring, quarter, width = sums_ref.shape
    heads, per_head, per_device, _ = query_ref.shape
    pairs = heads * HEAD_DIM // BLOCK
    copies = [
        pltpu.make_async_copy(ref, sums_ref.at[i], sum_sems.at[i]) for i, ref in enumerate(sums)
    ]
    copies.append(pltpu.make_async_copy(query_hbm, query_ref, sum_sems.at[count]))
    weight_copies = []
    for pair in range(pairs):
        at = pl.ds(pair * BLOCK, BLOCK)
        weight_copies.append(
            [
                pltpu.make_async_copy(hbm.at[:, at], ref.at[:, at], weight_sems.at[i, pair])
                for i, (hbm, ref) in enumerate(((key_hbm, key_ref), (value_hbm, value_ref)))
            ]
        )
    for copy in copies + weight_copies[0]:
        copy.start()
    for more in weight_copies[1:]:
        for copy in more:
            copy.start()
    rows = ring * quarter
    for half in range(2):
        for i in range(half * RING, (half + 1) * RING):
            copies[i].wait()
        summed = sums_ref[half * RING].astype(F32)
        for i in range(half * RING + 1, (half + 1) * RING):
            summed = summed + sums_ref[i].astype(F32)
        rows_ref[half * rows : (half + 1) * rows] = summed.astype(BF16).reshape(rows, width)
    copies[count].wait()
    many = per_head * per_device
    mine = (
        iota((many, 2 * rows), 0) % per_device // (per_device // 2)
        == iota((many, 2 * rows), 1) // rows
    )
    together = BLOCK // HEAD_DIM
    for pair in range(pairs):
        at = slice(pair * BLOCK, (pair + 1) * BLOCK)
        for copy in weight_copies[pair]:
            copy.wait()
        keys = jnp.dot(rows_ref[...], key_ref[:, at], preferred_element_type=F32)
        values = jnp.dot(rows_ref[...], value_ref[:, at], preferred_element_type=F32).astype(BF16)
        for place in range(together):
            head = pair * together + place
            at = slice(place * HEAD_DIM, (place + 1) * HEAD_DIM)
            key = keys[:, at]
            mean = jnp.mean(key * key, axis=-1, keepdims=True)
            key = (key / jnp.sqrt(mean + epsilon)).astype(BF16)
            query = query_ref[head].reshape(many, HEAD_DIM)
            scores = lax.dot_general(
                query, key, (((1,), (1,)), ((), ())), preferred_element_type=F32
            ) * HEAD_DIM ** (-0.5)
            weights = jnp.where(mine, jnp.exp(scores), 0.0)
            divisor = jnp.sum(weights, axis=-1, keepdims=True)
            numerator = jnp.dot(weights.astype(BF16), values[:, at], preferred_element_type=F32)
            out_ref[head] = (
                jnp.concatenate(
                    [numerator, jnp.broadcast_to(divisor, numerator.shape)], axis=1
                )
                .reshape(per_head, per_device, 2 * HEAD_DIM)
                .astype(BF16)
            )


def attend(sums, key_weight, value_weight, queries):
    shape = sums[0].shape
    _, quarter, width = shape
    heads, per_head, per_device, _ = queries.shape
    columns = key_weight.shape[1]
    return pl.pallas_call(
        attend_kernel,
        out_shape=jax.ShapeDtypeStruct((heads, per_head, per_device, 2 * HEAD_DIM), BF16),
        in_specs=[pl.BlockSpec(memory_space=pl.ANY)] * (len(sums) + 3),
        out_specs=VMEM,
        scratch_shapes=[
            pltpu.VMEM((len(sums),) + shape, BF16),
            pltpu.VMEM((2 * RING * quarter, width), BF16),
            pltpu.VMEM(key_weight.shape, BF16),
            pltpu.VMEM(value_weight.shape, BF16),
            pltpu.VMEM(queries.shape, BF16),
            pltpu.SemaphoreType.DMA((len(sums) + 1,)),
            pltpu.SemaphoreType.DMA((2, columns // BLOCK)),
        ],
        compiler_params=params(ATTEND_MIB),
        cost_estimate=pl.CostEstimate(
            flops=8 * RING * quarter * width * columns,
            bytes_accessed=4 * width * columns,
            transcendentals=0,
        ),
    )(*sums, key_weight, value_weight, queries)


def combine_kernel(at_ref, target_ref, packed_ref, own_ref, one_ref, two_ref, three_ref):
    target = target_ref[...]
    per_group = own_ref.shape[0] - TOTAL_ROWS
    for shift, ref in enumerate((own_ref, one_ref, two_ref, three_ref)):
        group = lax.rem(at_ref[0] + shift, RING)
        match = target == iota((target.shape[0], per_group), 1) + group * per_group
        summed = lax.dot_general(
            jnp.where(match, 1.0, 0.0).astype(BF16),
            packed_ref[...],
            (((0,), (0,)), ((), ())),
            preferred_element_type=F32,
        )
        ref[:per_group] = summed[:, :HEAD_DIM].astype(ref.dtype)
        totals = jnp.zeros((TOTAL_ROWS, HEAD_DIM), F32)
        for row, first in enumerate(range(0, per_group, HEAD_DIM)):
            part = summed[first : first + HEAD_DIM, HEAD_DIM:]
            lane = iota(part.shape, 0) == iota(part.shape, 1)
            part = jnp.sum(jnp.where(lane, part, 0.0), axis=0, keepdims=True)
            totals = jnp.where(iota(totals.shape, 0) == row, part, totals)
        ref[per_group:] = totals.astype(ref.dtype)


def combine(at, target, packed, per_group):
    shape = (per_group + TOTAL_ROWS, HEAD_DIM)
    sent = jax.ShapeDtypeStruct(shape, BF16)
    return pl.pallas_call(
        combine_kernel,
        out_shape=(jax.ShapeDtypeStruct(shape, F32), sent, sent, sent),
        in_specs=[SMEM, VMEM, VMEM],
        out_specs=(VMEM,) * 4,
        compiler_params=params(8),
    )(at, target, packed)


def project_kernel(core, at_ref, own_ref, one_ref, two_ref, three_ref, weight_ref, out_ref):
    summed = own_ref[...]
    for ref in (one_ref, two_ref, three_ref):
        summed = summed + ref[...].astype(F32)
    per_group = summed.shape[0] - TOTAL_ROWS
    attended = []
    for row, first in enumerate(range(0, per_group, HEAD_DIM)):
        part = summed[first : min(first + HEAD_DIM, per_group)]
        totals = jnp.broadcast_to(summed[per_group + row : per_group + row + 1], part.shape)
        lane = iota(part.shape, 0) == iota(part.shape, 1)
        divisor = jnp.sum(jnp.where(lane, totals, 0.0), axis=1, keepdims=True)
        attended.append(part / jnp.where(divisor > 0.0, divisor, 1.0))
    attended = jnp.concatenate(attended, axis=0)
    half = per_group // 2
    attended = jnp.concatenate([attended[:half], attended[half:]], axis=1).astype(BF16)
    here = at_ref[1]
    z_at, y_at, core_at = here // (RING * CORES), here // CORES % RING, here % CORES
    column = lax.rem(core_at + core, CORES)
    for z in range(RING):
        for y in range(RING):
            block = (
                lax.rem(z_at + z, RING) * RING + lax.rem(y_at + y, RING)
            ) * CORES + column
            at = pl.ds(pl.multiple_of(block * BLOCK, BLOCK), BLOCK)
            out_ref[z, y] = jnp.dot(
                attended, weight_ref[:, at], preferred_element_type=F32
            ).astype(BF16)


def project(at, own, received, weight, core):
    depth, columns = weight.shape
    rows = (own.shape[0] - TOTAL_ROWS) // 2
    return pl.pallas_call(
        functools.partial(project_kernel, core),
        out_shape=jax.ShapeDtypeStruct((RING, RING, rows, BLOCK), BF16),
        in_specs=[SMEM] + [VMEM] * 5,
        out_specs=VMEM,
        compiler_params=params(8),
        cost_estimate=pl.CostEstimate(
            flops=rows * depth * columns, bytes_accessed=2 * depth * columns, transcendentals=0
        ),
    )(at, own, *received, weight)


def first_sum_kernel(kept_ref, got_ref, own_ref, one_ref, two_ref, three_ref):
    for shift, ref in enumerate((own_ref, one_ref, two_ref, three_ref)):
        ref[...] = (kept_ref[shift].astype(F32) + got_ref[shift].astype(F32)).astype(ref.dtype)


def first_sum(kept, got):
    sent = jax.ShapeDtypeStruct(kept.shape[1:], BF16)
    return pl.pallas_call(
        first_sum_kernel,
        out_shape=(jax.ShapeDtypeStruct(kept.shape[1:], F32), sent, sent, sent),
        in_specs=[VMEM, VMEM],
        out_specs=(VMEM,) * 4,
        compiler_params=params(8),
    )(kept, got)


def second_sum_kernel(kept_ref, a_ref, b_ref, c_ref, own_ref, one_ref, two_ref, three_ref):
    for shift, ref in enumerate((own_ref, one_ref, two_ref, three_ref)):
        summed = kept_ref[shift]
        for got in (a_ref, b_ref, c_ref):
            summed = summed + got[shift].astype(F32)
        ref[...] = summed.astype(ref.dtype)


def second_sum(kept, got):
    sent = jax.ShapeDtypeStruct(kept.shape[1:], BF16)
    return pl.pallas_call(
        second_sum_kernel,
        out_shape=(jax.ShapeDtypeStruct(kept.shape[1:], F32), sent, sent, sent),
        in_specs=[VMEM] * 4,
        out_specs=(VMEM,) * 4,
        compiler_params=params(8),
    )(kept, *got)


def last_sum_kernel(kept_ref, a_ref, b_ref, c_ref, residual_ref, out_ref):
    summed = kept_ref[...]
    for got in (a_ref, b_ref, c_ref):
        summed = summed + got[...].astype(F32)
    out_ref[...] = (residual_ref[...].astype(F32) + summed.reshape(out_ref.shape)).astype(BF16)


def last_sum(kept, got, residual):
    return pl.pallas_call(
        last_sum_kernel,
        out_shape=jax.ShapeDtypeStruct(residual.shape, BF16),
        in_specs=[VMEM] * 5,
        out_specs=VMEM,
        compiler_params=params(8),
    )(kept, *got, residual)


def body(
    patches,
    enc_tiles,
    req_tiles,
    req_owner,
    fc1_weight,
    fc2_weight,
    key_weight,
    value_weight,
    query_weight,
    out_weight,
    text_hidden,
):
    capacity = patches.shape[0]
    devices = lax.axis_size("dev")
    local_heads = HEADS // devices
    slots, steps, model_width = text_hidden.shape
    dev_at = lax.axis_index("dev")
    at = jnp.stack([lax.axis_index("pool"), dev_at]).astype(jnp.int32)
    halves = capacity // RING

    own = [normalize(at, patches), second_half(at, text_hidden, query_weight, patches)]
    sources = [[rows] + [pool_shift(rows, s) for s in range(1, RING)] for rows in own]
    held = hold(fc1_weight, fc2_weight, sources[1][0])
    target = tables(
        at,
        enc_tiles.reshape(1, -1),
        req_tiles.reshape(1, -1),
        req_owner,
        slots,
        steps,
        local_heads,
        capacity,
        sources[1][0],
    )
    sums, queries = [], None
    for i in range(halves):
        total, *messages = feed_forward(
            at, patches, sources[i], fc1_weight, fc2_weight, i, (held, target)
        )
        queries = messages[-1]
        sums += [total] + [pool_shift(messages[s - 1], s) for s in range(1, RING)]
    chosen = select(at, target, queries, local_heads * slots * steps)
    per_device = halves * local_heads * steps
    tile_queries = lax.all_to_all(
        chosen.reshape(devices, per_device, HEAD_DIM), "dev", split_axis=0, concat_axis=0, tiled=True
    ).reshape(KV_HEADS, devices // KV_HEADS, per_device, HEAD_DIM)
    packed = attend(sums, key_weight, value_weight, tile_queries)
    packed = lax.all_to_all(
        packed.reshape(devices, per_device, 2 * HEAD_DIM),
        "dev",
        split_axis=0,
        concat_axis=0,
        tiled=True,
    ).reshape(devices * per_device, 2 * HEAD_DIM)
    summed, *messages = combine(at, target, packed, local_heads * slots * steps)
    received = [pool_shift(messages[s - 1], s) for s in range(1, RING)]

    away = dev_shift(project(at, summed, received, out_weight, 1), 0, 0, 1)
    kept = project(at, summed, received, out_weight, 0)
    kept, *messages = first_sum(kept, away)
    received = [dev_shift(messages[s - 1], s, 0, 0) for s in range(1, RING)]
    kept, *messages = second_sum(kept, received)
    received = [dev_shift(messages[s - 1], 0, s, 0) for s in range(1, RING)]
    width_out = model_width // devices
    residual = lax.dynamic_slice_in_dim(text_hidden, dev_at * width_out, width_out, 2)
    return last_sum(kept, received, residual)


def solution(mesh):
    return jax.shard_map(
        body,
        mesh=mesh,
        in_specs=(
            P("dev", "pool", None),
            P(),
            P(),
            P(),
            P(None, "pool"),
            P("pool", None),
            P(),
            P(),
            P(None, "dev"),
            P("dev", None),
            P("pool", None, None),
        ),
        out_specs=P("pool", None, "dev"),
        check_vma=False,
    )
```

```python
import functools

import jax
import jax.numpy as jnp
from jax import lax
from jax.experimental import pallas as pl
from jax.experimental.pallas import tpu as pltpu
from jax.sharding import PartitionSpec as P

HEADS = 64
KV_HEADS = 8
HEAD_DIM = 128
CORES = 2
RING = 4
BLOCK = 256
TOTAL_ROWS = 16
ATTEND_MIB = 20
F32, BF16 = jnp.float32, jnp.bfloat16

epsilon = 1e-05

VMEM = pl.BlockSpec(memory_space=pltpu.VMEM)
SMEM = pl.BlockSpec(memory_space=pltpu.SMEM)


def params(mib):
    return pltpu.CompilerParams(vmem_limit_bytes=mib * 1024 * 1024)


def pool_shift(x, by):
    return lax.ppermute(x, "pool", [(i, (i + by) % RING) for i in range(RING)])


def dev_shift(x, by_z, by_y, by_core):
    pairs = []
    for z in range(RING):
        for y in range(RING):
            for k in range(CORES):
                to = ((z + by_z) % RING, (y + by_y) % RING, (k + by_core) % CORES)
                pairs.append(((z * RING + y) * CORES + k, (to[0] * RING + to[1]) * CORES + to[2]))
    return lax.ppermute(x, "dev", pairs)


def layer_rows(values):
    center = values - jnp.mean(values, axis=-1, keepdims=True)
    spread = jnp.mean(center * center, axis=-1, keepdims=True)
    return (center / jnp.sqrt(spread + epsilon)).astype(BF16)


def normalize_kernel(half, at_ref, patches_ref, rows_ref):
    for r in range(RING):
        slot = lax.rem(at_ref[0] + r, RING) + half * RING
        rows_ref[r] = layer_rows(patches_ref[slot].astype(F32))


def normalize(at, patches):
    _, quarter, width = patches.shape
    return pl.pallas_call(
        functools.partial(normalize_kernel, 0),
        out_shape=jax.ShapeDtypeStruct((RING, quarter, width), BF16),
        in_specs=[SMEM, VMEM],
        out_specs=VMEM,
        compiler_params=params(8),
    )(at, patches)


def hold_kernel(one_ref, two_ref, _, out_ref):
    out_ref[...] = jnp.zeros_like(out_ref)


def hold(one, two, after):
    return pl.pallas_call(
        hold_kernel,
        out_shape=jax.ShapeDtypeStruct((8, 128), F32),
        in_specs=[VMEM, VMEM, pl.BlockSpec(memory_space=pl.ANY)],
        out_specs=VMEM,
        compiler_params=params(8),
    )(one, two, after)


def feed_forward_kernel(
    half, at_ref, patches_ref, own_rows, one_rows, two_rows, three_rows, fc1_ref, fc2_ref, *refs
):
    total_ref, one_ref, two_ref, three_ref, *query_refs, rows_ref, wide_ref = refs[2:]
    for ref in query_refs:
        for source, rows in enumerate((own_rows, one_rows, two_rows, three_rows)):
            ref[source] = rows[RING]
    hidden, width = fc2_ref.shape
    quarter = patches_ref.shape[1]
    rows = RING * quarter
    for source, ref in enumerate((own_rows, one_rows, two_rows, three_rows)):
        rows_ref[source * rows : (source + 1) * rows] = ref[:RING].reshape(rows, width)
    for step in range(hidden // BLOCK):
        at = slice(step * BLOCK, (step + 1) * BLOCK)
        values = jnp.dot(rows_ref[...], fc1_ref[:, at], preferred_element_type=F32)
        wide_ref[:, at] = (0.5 * values * (1.0 + lax.erf(values * 0.5**0.5))).astype(BF16)
    outs = (total_ref, one_ref, two_ref, three_ref)
    for step in range(width // BLOCK):
        at = slice(step * BLOCK, (step + 1) * BLOCK)
        sums = jnp.dot(wide_ref[...], fc2_ref[:, at], preferred_element_type=F32)
        for source in range(RING):
            for m in range(RING):
                piece = sums[source * rows + m * quarter : source * rows + (m + 1) * quarter]
                shift = (m - source) % RING
                if source == 0:
                    slot = lax.rem(at_ref[0] + m, RING) + half * RING
                    piece = piece + patches_ref[slot, :, at].astype(F32)
                outs[shift][m, :, at] = piece.astype(outs[shift].dtype)


def feed_forward(at, patches, sources, fc1, fc2, half, after):
    _, quarter, width = patches.shape
    hidden = fc1.shape[1]
    shape = (RING, quarter, width)
    sent = jax.ShapeDtypeStruct(shape, BF16)
    return pl.pallas_call(
        functools.partial(feed_forward_kernel, half),
        out_shape=(sent,) * (4 + half),
        in_specs=[SMEM] + [VMEM] * (7 + len(after)),
        out_specs=(VMEM,) * (4 + half),
        scratch_shapes=[
            pltpu.VMEM((RING * RING * quarter, width), BF16),
            pltpu.VMEM((RING * RING * quarter, hidden), BF16),
        ],
        compiler_params=params(14),
        cost_estimate=pl.CostEstimate(
            flops=4 * RING * RING * quarter * width * hidden,
            bytes_accessed=4 * width * hidden,
            transcendentals=0,
        ),
    )(at, patches, *sources, fc1, fc2, *after)


def pair_sum_kernel(a_ref, b_ref, out_ref):
    out_ref[...] = (a_ref[...].astype(F32) + b_ref[...].astype(F32)).astype(BF16)


def pair_sum(a, b):
    return pl.pallas_call(
        pair_sum_kernel,
        out_shape=jax.ShapeDtypeStruct(a.shape, BF16),
        in_specs=[VMEM, VMEM],
        out_specs=VMEM,
        compiler_params=params(8),
    )(a, b)


def query_kernel(at_ref, text_ref, weight_ref, patches_ref, sent_ref, total_ref, square_ref):
    step = pl.program_id(0)
    rows, columns = total_ref.shape

    @pl.when(step == 0)
    def _():
        total_ref[...] = jnp.zeros_like(total_ref)
        square_ref[...] = jnp.zeros_like(square_ref)

    slot = lax.rem(at_ref[0] + step, RING) + RING
    sent_ref[step] = layer_rows(patches_ref[slot].astype(F32))
    text = text_ref[...].reshape(rows, text_ref.shape[-1])
    total_ref[...] += jnp.dot(text, weight_ref[...], preferred_element_type=F32)
    wide = text.astype(F32)
    square_ref[...] += jnp.sum(wide * wide, axis=-1, keepdims=True)

    @pl.when(step == pl.num_programs(0) - 1)
    def _():
        width = text_ref.shape[-1] * pl.num_programs(0)
        values = total_ref[...] / jnp.sqrt(square_ref[...] / width + epsilon)
        quarter = sent_ref.shape[1]
        for head in range(columns // HEAD_DIM):
            part = values[:, head * HEAD_DIM : (head + 1) * HEAD_DIM]
            mean = jnp.mean(part * part, axis=-1, keepdims=True)
            part = (part / jnp.sqrt(mean + epsilon)).astype(BF16)
            for piece in range(rows // quarter):
                lane = (head * (rows // quarter) + piece) * HEAD_DIM
                sent_ref[RING, :, lane : lane + HEAD_DIM] = part[
                    piece * quarter : (piece + 1) * quarter
                ]
        filled = columns // HEAD_DIM * (rows // quarter) * HEAD_DIM
        sent_ref[RING, :, filled:] = jnp.zeros((quarter, sent_ref.shape[2] - filled), BF16)


def second_half(at, text, weight, patches):
    slots, steps, model = text.shape
    rows = slots * steps
    _, quarter, width = patches.shape
    columns = weight.shape[1]
    depth = model // RING
    return pl.pallas_call(
        query_kernel,
        grid=(RING,),
        out_shape=jax.ShapeDtypeStruct((RING + 1, quarter, width), BF16),
        in_specs=[
            SMEM,
            pl.BlockSpec((slots, steps, depth), lambda k: (0, 0, k)),
            pl.BlockSpec((depth, columns), lambda k: (k, 0)),
            pl.BlockSpec(patches.shape, lambda k: (0, 0, 0)),
        ],
        out_specs=pl.BlockSpec((RING + 1, quarter, width), lambda k: (0, 0, 0)),
        scratch_shapes=[pltpu.VMEM((rows, columns), F32), pltpu.VMEM((rows, 1), F32)],
        compiler_params=params(12),
        cost_estimate=pl.CostEstimate(
            flops=2 * rows * model * columns,
            bytes_accessed=2 * model * (columns + rows),
            transcendentals=0,
        ),
    )(at, text, weight, patches)


def iota(shape, dim):
    return lax.broadcasted_iota(jnp.int32, shape, dim)


def tables_kernel(
    slots, steps, heads, capacity, at_ref, enc_ref, req_ref, owner_ref, _, target_ref
):
    columns, requests = enc_ref.shape[1], req_ref.shape[1]
    halves = capacity // RING
    per_group = heads * slots * steps
    rows = target_ref.shape[0]
    before = iota((requests, requests), 0) < iota((requests, requests), 1)
    equal = iota((requests, requests), 0) == iota((requests, requests), 1)
    req_row = req_ref[...]
    req_column = jnp.sum(jnp.where(equal, req_row, 0), axis=1, keepdims=True)
    req_start = jnp.sum(jnp.where(before, req_column, 0), axis=0, keepdims=True)
    owner_column = owner_ref[...]
    owner_row = jnp.sum(jnp.where(equal, owner_column, 0), axis=0, keepdims=True)
    rank = jnp.sum(
        jnp.where(before & (owner_column == owner_row), 1, 0), axis=0, keepdims=True
    )
    place = owner_row * per_group + rank * steps
    enc_row = enc_ref[...]
    enc_equal = iota((columns, columns), 0) == iota((columns, columns), 1)
    enc_before = iota((columns, columns), 0) < iota((columns, columns), 1)
    enc_column = jnp.sum(jnp.where(enc_equal, enc_row, 0), axis=1, keepdims=True)
    enc_start = jnp.sum(jnp.where(enc_before, enc_column, 0), axis=0, keepdims=True)

    row = iota((rows, 1), 0)
    per_tile = heads * steps
    column = row // (halves * per_tile)
    slot = row // per_tile % halves * RING + at_ref[0]
    within = row % per_tile
    hit = column == iota((rows, columns), 1)
    count = jnp.sum(jnp.where(hit, enc_row, 0), axis=1, keepdims=True)
    start = jnp.sum(jnp.where(hit, enc_start, 0), axis=1, keepdims=True)
    tile = jnp.where(slot < count, start + slot, -1)
    has = (req_start <= tile) & (tile < req_start + req_row)
    base = jnp.sum(jnp.where(has, place + 1, 0), axis=1, keepdims=True) - 1
    target_ref[...] = jnp.where(
        base < 0, -1, base + within // steps * (slots * steps) + within % steps
    )


def tables(at, enc, req, owner, slots, steps, heads, capacity, after):
    rows = enc.shape[1] * (capacity // RING) * heads * steps
    return pl.pallas_call(
        functools.partial(tables_kernel, slots, steps, heads, capacity),
        out_shape=jax.ShapeDtypeStruct((rows, 1), jnp.int32),
        in_specs=[SMEM] + [VMEM] * 3 + [pl.BlockSpec(memory_space=pl.ANY)],
        out_specs=VMEM,
        compiler_params=params(8),
    )(at, enc, req, owner, after)


def select_kernel(per_group, at_ref, target_ref, sources_ref, chosen_ref):
    target = target_ref[...]
    chosen = jnp.zeros(chosen_ref.shape, F32)
    for shift in range(RING):
        group = lax.rem(at_ref[0] - shift + RING, RING)
        match = target == iota((target.shape[0], per_group), 1) + group * per_group
        pieces = per_group // sources_ref.shape[1]
        queries = jnp.concatenate(
            [
                sources_ref[shift, :, i * HEAD_DIM : (i + 1) * HEAD_DIM]
                for i in range(pieces)
            ],
            axis=0,
        )
        chosen = chosen + jnp.dot(
            jnp.where(match, 1.0, 0.0).astype(BF16), queries, preferred_element_type=F32
        )
    chosen_ref[...] = chosen.astype(BF16)


def select(at, target, sources, per_group):
    return pl.pallas_call(
        functools.partial(select_kernel, per_group),
        out_shape=jax.ShapeDtypeStruct((target.shape[0], HEAD_DIM), BF16),
        in_specs=[SMEM, VMEM, VMEM],
        out_specs=VMEM,
        compiler_params=params(8),
    )(at, target, sources)


def attend_kernel(*refs):
    count = 2 * RING - 1
    sums, (key_hbm, value_hbm, query_hbm) = refs[:count], refs[count : count + 3]
    out_ref, sums_ref, rows_ref, key_ref, value_ref, query_ref, sum_sems, weight_sems = refs[count + 3 :]
    _, ring, quarter, width = sums_ref.shape
    heads, per_head, per_device, _ = query_ref.shape
    pairs = heads * HEAD_DIM // BLOCK
    copies = [
        pltpu.make_async_copy(ref, sums_ref.at[i], sum_sems.at[i]) for i, ref in enumerate(sums)
    ]
    copies.append(pltpu.make_async_copy(query_hbm, query_ref, sum_sems.at[count]))
    weight_copies = []
    for pair in range(pairs):
        at = pl.ds(pair * BLOCK, BLOCK)
        weight_copies.append(
            [
                pltpu.make_async_copy(hbm.at[:, at], ref.at[:, at], weight_sems.at[i, pair])
                for i, (hbm, ref) in enumerate(((key_hbm, key_ref), (value_hbm, value_ref)))
            ]
        )
    for copy in copies + weight_copies[0]:
        copy.start()
    for more in weight_copies[1:]:
        for copy in more:
            copy.start()
    rows = ring * quarter
    for half, (first, last) in enumerate(((0, RING - 1), (RING - 1, count))):
        for i in range(first, last):
            copies[i].wait()
        summed = sums_ref[first].astype(F32)
        for i in range(first + 1, last):
            summed = summed + sums_ref[i].astype(F32)
        rows_ref[half * rows : (half + 1) * rows] = summed.astype(BF16).reshape(rows, width)
    copies[count].wait()
    many = per_head * per_device
    mine = (
        iota((many, 2 * rows), 0) % per_device // (per_device // 2)
        == iota((many, 2 * rows), 1) // rows
    )
    together = BLOCK // HEAD_DIM
    for pair in range(pairs):
        at = slice(pair * BLOCK, (pair + 1) * BLOCK)
        for copy in weight_copies[pair]:
            copy.wait()
        keys = jnp.dot(rows_ref[...], key_ref[:, at], preferred_element_type=F32)
        values = jnp.dot(rows_ref[...], value_ref[:, at], preferred_element_type=F32).astype(BF16)
        for place in range(together):
            head = pair * together + place
            at = slice(place * HEAD_DIM, (place + 1) * HEAD_DIM)
            key = keys[:, at]
            mean = jnp.mean(key * key, axis=-1, keepdims=True)
            key = (key / jnp.sqrt(mean + epsilon)).astype(BF16)
            query = query_ref[head].reshape(many, HEAD_DIM)
            scores = lax.dot_general(
                query, key, (((1,), (1,)), ((), ())), preferred_element_type=F32
            ) * HEAD_DIM ** (-0.5)
            weights = jnp.where(mine, jnp.exp(scores), 0.0)
            divisor = jnp.sum(weights, axis=-1, keepdims=True)
            numerator = jnp.dot(weights.astype(BF16), values[:, at], preferred_element_type=F32)
            out_ref[head] = (
                jnp.concatenate(
                    [numerator, jnp.broadcast_to(divisor, numerator.shape)], axis=1
                )
                .reshape(per_head, per_device, 2 * HEAD_DIM)
                .astype(BF16)
            )


def attend(sums, key_weight, value_weight, queries):
    shape = sums[0].shape
    _, quarter, width = shape
    heads, per_head, per_device, _ = queries.shape
    columns = key_weight.shape[1]
    return pl.pallas_call(
        attend_kernel,
        out_shape=jax.ShapeDtypeStruct((heads, per_head, per_device, 2 * HEAD_DIM), BF16),
        in_specs=[pl.BlockSpec(memory_space=pl.ANY)] * (len(sums) + 3),
        out_specs=VMEM,
        scratch_shapes=[
            pltpu.VMEM((len(sums),) + shape, BF16),
            pltpu.VMEM((2 * RING * quarter, width), BF16),
            pltpu.VMEM(key_weight.shape, BF16),
            pltpu.VMEM(value_weight.shape, BF16),
            pltpu.VMEM(queries.shape, BF16),
            pltpu.SemaphoreType.DMA((len(sums) + 1,)),
            pltpu.SemaphoreType.DMA((2, columns // BLOCK)),
        ],
        compiler_params=params(ATTEND_MIB),
        cost_estimate=pl.CostEstimate(
            flops=8 * RING * quarter * width * columns,
            bytes_accessed=4 * width * columns,
            transcendentals=0,
        ),
    )(*sums, key_weight, value_weight, queries)


def combine_kernel(at_ref, target_ref, packed_ref, own_ref, one_ref, two_ref, three_ref):
    target = target_ref[...]
    per_group = own_ref.shape[0] - TOTAL_ROWS
    for shift, ref in enumerate((own_ref, one_ref, two_ref, three_ref)):
        group = lax.rem(at_ref[0] + shift, RING)
        match = target == iota((target.shape[0], per_group), 1) + group * per_group
        summed = lax.dot_general(
            jnp.where(match, 1.0, 0.0).astype(BF16),
            packed_ref[...],
            (((0,), (0,)), ((), ())),
            preferred_element_type=F32,
        )
        ref[:per_group] = summed[:, :HEAD_DIM].astype(ref.dtype)
        totals = jnp.zeros((TOTAL_ROWS, HEAD_DIM), F32)
        for row, first in enumerate(range(0, per_group, HEAD_DIM)):
            part = summed[first : first + HEAD_DIM, HEAD_DIM:]
            lane = iota(part.shape, 0) == iota(part.shape, 1)
            part = jnp.sum(jnp.where(lane, part, 0.0), axis=0, keepdims=True)
            totals = jnp.where(iota(totals.shape, 0) == row, part, totals)
        ref[per_group:] = totals.astype(ref.dtype)


def combine(at, target, packed, per_group):
    shape = (per_group + TOTAL_ROWS, HEAD_DIM)
    sent = jax.ShapeDtypeStruct(shape, BF16)
    return pl.pallas_call(
        combine_kernel,
        out_shape=(jax.ShapeDtypeStruct(shape, F32), sent, sent, sent),
        in_specs=[SMEM, VMEM, VMEM],
        out_specs=(VMEM,) * 4,
        compiler_params=params(8),
    )(at, target, packed)


def project_kernel(core, at_ref, own_ref, one_ref, two_ref, three_ref, weight_ref, out_ref):
    summed = own_ref[...]
    for ref in (one_ref, two_ref, three_ref):
        summed = summed + ref[...].astype(F32)
    per_group = summed.shape[0] - TOTAL_ROWS
    attended = []
    for row, first in enumerate(range(0, per_group, HEAD_DIM)):
        part = summed[first : min(first + HEAD_DIM, per_group)]
        totals = jnp.broadcast_to(summed[per_group + row : per_group + row + 1], part.shape)
        lane = iota(part.shape, 0) == iota(part.shape, 1)
        divisor = jnp.sum(jnp.where(lane, totals, 0.0), axis=1, keepdims=True)
        attended.append(part / jnp.where(divisor > 0.0, divisor, 1.0))
    attended = jnp.concatenate(attended, axis=0)
    half = per_group // 2
    attended = jnp.concatenate([attended[:half], attended[half:]], axis=1).astype(BF16)
    here = at_ref[1]
    z_at, y_at, core_at = here // (RING * CORES), here // CORES % RING, here % CORES
    column = lax.rem(core_at + core, CORES)
    for z in range(RING):
        for y in range(RING):
            block = (
                lax.rem(z_at + z, RING) * RING + lax.rem(y_at + y, RING)
            ) * CORES + column
            at = pl.ds(pl.multiple_of(block * BLOCK, BLOCK), BLOCK)
            out_ref[z, y] = jnp.dot(
                attended, weight_ref[:, at], preferred_element_type=F32
            ).astype(BF16)


def project(at, own, received, weight, core):
    depth, columns = weight.shape
    rows = (own.shape[0] - TOTAL_ROWS) // 2
    return pl.pallas_call(
        functools.partial(project_kernel, core),
        out_shape=jax.ShapeDtypeStruct((RING, RING, rows, BLOCK), BF16),
        in_specs=[SMEM] + [VMEM] * 5,
        out_specs=VMEM,
        compiler_params=params(8),
        cost_estimate=pl.CostEstimate(
            flops=rows * depth * columns, bytes_accessed=2 * depth * columns, transcendentals=0
        ),
    )(at, own, *received, weight)


def first_sum_kernel(kept_ref, got_ref, own_ref, one_ref, two_ref, three_ref):
    for shift, ref in enumerate((own_ref, one_ref, two_ref, three_ref)):
        ref[...] = (kept_ref[shift].astype(F32) + got_ref[shift].astype(F32)).astype(ref.dtype)


def first_sum(kept, got):
    sent = jax.ShapeDtypeStruct(kept.shape[1:], BF16)
    return pl.pallas_call(
        first_sum_kernel,
        out_shape=(jax.ShapeDtypeStruct(kept.shape[1:], F32), sent, sent, sent),
        in_specs=[VMEM, VMEM],
        out_specs=(VMEM,) * 4,
        compiler_params=params(8),
    )(kept, got)


def second_sum_kernel(kept_ref, a_ref, b_ref, c_ref, own_ref, one_ref, two_ref, three_ref):
    for shift, ref in enumerate((own_ref, one_ref, two_ref, three_ref)):
        summed = kept_ref[shift]
        for got in (a_ref, b_ref, c_ref):
            summed = summed + got[shift].astype(F32)
        ref[...] = summed.astype(ref.dtype)


def second_sum(kept, got):
    sent = jax.ShapeDtypeStruct(kept.shape[1:], BF16)
    return pl.pallas_call(
        second_sum_kernel,
        out_shape=(jax.ShapeDtypeStruct(kept.shape[1:], F32), sent, sent, sent),
        in_specs=[VMEM] * 4,
        out_specs=(VMEM,) * 4,
        compiler_params=params(8),
    )(kept, *got)


def last_sum_kernel(kept_ref, a_ref, b_ref, c_ref, residual_ref, out_ref):
    summed = kept_ref[...]
    for got in (a_ref, b_ref, c_ref):
        summed = summed + got[...].astype(F32)
    out_ref[...] = (residual_ref[...].astype(F32) + summed.reshape(out_ref.shape)).astype(BF16)


def last_sum(kept, got, residual):
    return pl.pallas_call(
        last_sum_kernel,
        out_shape=jax.ShapeDtypeStruct(residual.shape, BF16),
        in_specs=[VMEM] * 5,
        out_specs=VMEM,
        compiler_params=params(8),
    )(kept, *got, residual)


def body(
    patches,
    enc_tiles,
    req_tiles,
    req_owner,
    fc1_weight,
    fc2_weight,
    key_weight,
    value_weight,
    query_weight,
    out_weight,
    text_hidden,
):
    capacity = patches.shape[0]
    devices = lax.axis_size("dev")
    local_heads = HEADS // devices
    slots, steps, model_width = text_hidden.shape
    dev_at = lax.axis_index("dev")
    at = jnp.stack([lax.axis_index("pool"), dev_at]).astype(jnp.int32)
    halves = capacity // RING

    own = [normalize(at, patches), second_half(at, text_hidden, query_weight, patches)]
    sources = [[rows] + [pool_shift(rows, s) for s in range(1, RING)] for rows in own]
    held = hold(fc1_weight, fc2_weight, sources[1][0])
    target = tables(
        at,
        enc_tiles.reshape(1, -1),
        req_tiles.reshape(1, -1),
        req_owner,
        slots,
        steps,
        local_heads,
        capacity,
        sources[1][0],
    )
    sums, queries = [], None
    for i in range(halves):
        total, *messages = feed_forward(
            at, patches, sources[i], fc1_weight, fc2_weight, i, (held, target)
        )
        queries = messages[-1]
        if i == 0:
            near = pair_sum(messages[0], pool_shift(messages[1], 1))
            sums += [total, pool_shift(messages[2], -1), pool_shift(near, 1)]
        else:
            sums += [total] + [pool_shift(messages[s - 1], s) for s in range(1, RING)]
    chosen = select(at, target, queries, local_heads * slots * steps)
    per_device = halves * local_heads * steps
    tile_queries = lax.all_to_all(
        chosen.reshape(devices, per_device, HEAD_DIM), "dev", split_axis=0, concat_axis=0, tiled=True
    ).reshape(KV_HEADS, devices // KV_HEADS, per_device, HEAD_DIM)
    packed = attend(sums, key_weight, value_weight, tile_queries)
    packed = lax.all_to_all(
        packed.reshape(devices, per_device, 2 * HEAD_DIM),
        "dev",
        split_axis=0,
        concat_axis=0,
        tiled=True,
    ).reshape(devices * per_device, 2 * HEAD_DIM)
    summed, *messages = combine(at, target, packed, local_heads * slots * steps)
    received = [pool_shift(messages[s - 1], s) for s in range(1, RING)]

    away = dev_shift(project(at, summed, received, out_weight, 1), 0, 0, 1)
    kept = project(at, summed, received, out_weight, 0)
    kept, *messages = first_sum(kept, away)
    received = [dev_shift(messages[s - 1], s, 0, 0) for s in range(1, RING)]
    kept, *messages = second_sum(kept, received)
    received = [dev_shift(messages[s - 1], 0, s, 0) for s in range(1, RING)]
    width_out = model_width // devices
    residual = lax.dynamic_slice_in_dim(text_hidden, dev_at * width_out, width_out, 2)
    return last_sum(kept, received, residual)


def solution(mesh):
    return jax.shard_map(
        body,
        mesh=mesh,
        in_specs=(
            P("dev", "pool", None),
            P(),
            P(),
            P(),
            P(None, "pool"),
            P("pool", None),
            P(),
            P(),
            P(None, "dev"),
            P("dev", None),
            P("pool", None, None),
        ),
        out_specs=P("pool", None, "dev"),
        check_vma=False,
    )
```

```python
import functools

import jax
import jax.numpy as jnp
from jax import lax
from jax.experimental import pallas as pl
from jax.experimental.pallas import tpu as pltpu
from jax.sharding import PartitionSpec as P

HEADS = 64
KV_HEADS = 8
HEAD_DIM = 128
CORES = 2
RING = 4
BLOCK = 256
TOTAL_ROWS = 16
ATTEND_MIB = 20
F32, BF16 = jnp.float32, jnp.bfloat16

epsilon = 1e-05

VMEM = pl.BlockSpec(memory_space=pltpu.VMEM)
SMEM = pl.BlockSpec(memory_space=pltpu.SMEM)


def params(mib):
    return pltpu.CompilerParams(vmem_limit_bytes=mib * 1024 * 1024)


def pool_shift(x, by):
    return lax.ppermute(x, "pool", [(i, (i + by) % RING) for i in range(RING)])


def dev_shift(x, by_z, by_y, by_core):
    pairs = []
    for z in range(RING):
        for y in range(RING):
            for k in range(CORES):
                to = ((z + by_z) % RING, (y + by_y) % RING, (k + by_core) % CORES)
                pairs.append(((z * RING + y) * CORES + k, (to[0] * RING + to[1]) * CORES + to[2]))
    return lax.ppermute(x, "dev", pairs)


def layer_rows(values):
    center = values - jnp.mean(values, axis=-1, keepdims=True)
    spread = jnp.mean(center * center, axis=-1, keepdims=True)
    return (center / jnp.sqrt(spread + epsilon)).astype(BF16)


def normalize_kernel(half, at_ref, patches_ref, rows_ref):
    for r in range(RING):
        slot = lax.rem(at_ref[0] + r, RING) + half * RING
        rows_ref[r] = layer_rows(patches_ref[slot].astype(F32))


def normalize(at, patches):
    _, quarter, width = patches.shape
    return pl.pallas_call(
        functools.partial(normalize_kernel, 0),
        out_shape=jax.ShapeDtypeStruct((RING, quarter, width), BF16),
        in_specs=[SMEM, VMEM],
        out_specs=VMEM,
        compiler_params=params(8),
    )(at, patches)


def hold_kernel(one_ref, two_ref, _, out_ref):
    out_ref[...] = jnp.zeros_like(out_ref)


def hold(one, two, after):
    return pl.pallas_call(
        hold_kernel,
        out_shape=jax.ShapeDtypeStruct((8, 128), F32),
        in_specs=[VMEM, VMEM, pl.BlockSpec(memory_space=pl.ANY)],
        out_specs=VMEM,
        compiler_params=params(8),
    )(one, two, after)


def feed_forward_kernel(
    half, at_ref, patches_ref, own_rows, one_rows, two_rows, three_rows, fc1_ref, fc2_ref, *refs
):
    total_ref, one_ref, two_ref, three_ref, *query_refs, rows_ref, wide_ref = refs[2:]
    for ref in query_refs:
        for source, rows in enumerate((own_rows, one_rows, two_rows, three_rows)):
            ref[source] = rows[RING]
    hidden, width = fc2_ref.shape
    quarter = patches_ref.shape[1]
    rows = RING * quarter
    for source, ref in enumerate((own_rows, one_rows, two_rows, three_rows)):
        rows_ref[source * rows : (source + 1) * rows] = ref[:RING].reshape(rows, width)
    for step in range(hidden // BLOCK):
        at = slice(step * BLOCK, (step + 1) * BLOCK)
        values = jnp.dot(rows_ref[...], fc1_ref[:, at], preferred_element_type=F32)
        wide_ref[:, at] = (0.5 * values * (1.0 + lax.erf(values * 0.5**0.5))).astype(BF16)
    outs = (total_ref, one_ref, two_ref, three_ref)
    for step in range(width // BLOCK):
        at = slice(step * BLOCK, (step + 1) * BLOCK)
        sums = jnp.dot(wide_ref[...], fc2_ref[:, at], preferred_element_type=F32)
        for source in range(RING):
            for m in range(RING):
                piece = sums[source * rows + m * quarter : source * rows + (m + 1) * quarter]
                shift = (m - source) % RING
                if source == 0:
                    slot = lax.rem(at_ref[0] + m, RING) + half * RING
                    piece = piece + patches_ref[slot, :, at].astype(F32)
                outs[shift][m, :, at] = piece.astype(outs[shift].dtype)


def feed_forward(at, patches, sources, fc1, fc2, half, after):
    _, quarter, width = patches.shape
    hidden = fc1.shape[1]
    shape = (RING, quarter, width)
    sent = jax.ShapeDtypeStruct(shape, BF16)
    return pl.pallas_call(
        functools.partial(feed_forward_kernel, half),
        out_shape=(sent,) * (4 + half),
        in_specs=[SMEM] + [VMEM] * (7 + len(after)),
        out_specs=(VMEM,) * (4 + half),
        scratch_shapes=[
            pltpu.VMEM((RING * RING * quarter, width), BF16),
            pltpu.VMEM((RING * RING * quarter, hidden), BF16),
        ],
        compiler_params=params(14),
        cost_estimate=pl.CostEstimate(
            flops=4 * RING * RING * quarter * width * hidden,
            bytes_accessed=4 * width * hidden,
            transcendentals=0,
        ),
    )(at, patches, *sources, fc1, fc2, *after)


def pair_sum_kernel(a_ref, b_ref, out_ref):
    out_ref[...] = (a_ref[...].astype(F32) + b_ref[...].astype(F32)).astype(BF16)


def pair_sum(a, b):
    return pl.pallas_call(
        pair_sum_kernel,
        out_shape=jax.ShapeDtypeStruct(a.shape, BF16),
        in_specs=[VMEM, VMEM],
        out_specs=VMEM,
        compiler_params=params(8),
    )(a, b)


def query_kernel(at_ref, text_ref, weight_ref, patches_ref, sent_ref, total_ref, square_ref):
    step = pl.program_id(0)
    rows, columns = total_ref.shape

    @pl.when(step == 0)
    def _():
        total_ref[...] = jnp.zeros_like(total_ref)
        square_ref[...] = jnp.zeros_like(square_ref)

    slot = lax.rem(at_ref[0] + step, RING) + RING
    sent_ref[step] = layer_rows(patches_ref[slot].astype(F32))
    text = text_ref[...].reshape(rows, text_ref.shape[-1])
    total_ref[...] += jnp.dot(text, weight_ref[...], preferred_element_type=F32)
    wide = text.astype(F32)
    square_ref[...] += jnp.sum(wide * wide, axis=-1, keepdims=True)

    @pl.when(step == pl.num_programs(0) - 1)
    def _():
        width = text_ref.shape[-1] * pl.num_programs(0)
        values = total_ref[...] / jnp.sqrt(square_ref[...] / width + epsilon)
        quarter = sent_ref.shape[1]
        for head in range(columns // HEAD_DIM):
            part = values[:, head * HEAD_DIM : (head + 1) * HEAD_DIM]
            mean = jnp.mean(part * part, axis=-1, keepdims=True)
            part = (part / jnp.sqrt(mean + epsilon)).astype(BF16)
            for piece in range(rows // quarter):
                lane = (head * (rows // quarter) + piece) * HEAD_DIM
                sent_ref[RING, :, lane : lane + HEAD_DIM] = part[
                    piece * quarter : (piece + 1) * quarter
                ]
        filled = columns // HEAD_DIM * (rows // quarter) * HEAD_DIM
        sent_ref[RING, :, filled:] = jnp.zeros((quarter, sent_ref.shape[2] - filled), BF16)


def second_half(at, text, weight, patches):
    slots, steps, model = text.shape
    rows = slots * steps
    _, quarter, width = patches.shape
    columns = weight.shape[1]
    depth = model // RING
    return pl.pallas_call(
        query_kernel,
        grid=(RING,),
        out_shape=jax.ShapeDtypeStruct((RING + 1, quarter, width), BF16),
        in_specs=[
            SMEM,
            pl.BlockSpec((slots, steps, depth), lambda k: (0, 0, k)),
            pl.BlockSpec((depth, columns), lambda k: (k, 0)),
            pl.BlockSpec(patches.shape, lambda k: (0, 0, 0)),
        ],
        out_specs=pl.BlockSpec((RING + 1, quarter, width), lambda k: (0, 0, 0)),
        scratch_shapes=[pltpu.VMEM((rows, columns), F32), pltpu.VMEM((rows, 1), F32)],
        compiler_params=params(12),
        cost_estimate=pl.CostEstimate(
            flops=2 * rows * model * columns,
            bytes_accessed=2 * model * (columns + rows),
            transcendentals=0,
        ),
    )(at, text, weight, patches)


def iota(shape, dim):
    return lax.broadcasted_iota(jnp.int32, shape, dim)


def tables_kernel(
    slots, steps, heads, capacity, at_ref, enc_ref, req_ref, owner_ref, _, target_ref
):
    columns, requests = enc_ref.shape[1], req_ref.shape[1]
    halves = capacity // RING
    per_group = heads * slots * steps
    rows = target_ref.shape[0]
    before = iota((requests, requests), 0) < iota((requests, requests), 1)
    equal = iota((requests, requests), 0) == iota((requests, requests), 1)
    req_row = req_ref[...]
    req_column = jnp.sum(jnp.where(equal, req_row, 0), axis=1, keepdims=True)
    req_start = jnp.sum(jnp.where(before, req_column, 0), axis=0, keepdims=True)
    owner_column = owner_ref[...]
    owner_row = jnp.sum(jnp.where(equal, owner_column, 0), axis=0, keepdims=True)
    rank = jnp.sum(
        jnp.where(before & (owner_column == owner_row), 1, 0), axis=0, keepdims=True
    )
    place = owner_row * per_group + rank * steps
    enc_row = enc_ref[...]
    enc_equal = iota((columns, columns), 0) == iota((columns, columns), 1)
    enc_before = iota((columns, columns), 0) < iota((columns, columns), 1)
    enc_column = jnp.sum(jnp.where(enc_equal, enc_row, 0), axis=1, keepdims=True)
    enc_start = jnp.sum(jnp.where(enc_before, enc_column, 0), axis=0, keepdims=True)

    row = iota((rows, 1), 0)
    per_tile = heads * steps
    column = row // (halves * per_tile)
    slot = row // per_tile % halves * RING + at_ref[0]
    within = row % per_tile
    hit = column == iota((rows, columns), 1)
    count = jnp.sum(jnp.where(hit, enc_row, 0), axis=1, keepdims=True)
    start = jnp.sum(jnp.where(hit, enc_start, 0), axis=1, keepdims=True)
    tile = jnp.where(slot < count, start + slot, -1)
    has = (req_start <= tile) & (tile < req_start + req_row)
    base = jnp.sum(jnp.where(has, place + 1, 0), axis=1, keepdims=True) - 1
    target_ref[...] = jnp.where(
        base < 0, -1, base + within // steps * (slots * steps) + within % steps
    )


def tables(at, enc, req, owner, slots, steps, heads, capacity, after):
    rows = enc.shape[1] * (capacity // RING) * heads * steps
    return pl.pallas_call(
        functools.partial(tables_kernel, slots, steps, heads, capacity),
        out_shape=jax.ShapeDtypeStruct((rows, 1), jnp.int32),
        in_specs=[SMEM] + [VMEM] * 3 + [pl.BlockSpec(memory_space=pl.ANY)],
        out_specs=VMEM,
        compiler_params=params(8),
    )(at, enc, req, owner, after)


def select_kernel(per_group, at_ref, target_ref, sources_ref, chosen_ref):
    target = target_ref[...]
    chosen = jnp.zeros(chosen_ref.shape, F32)
    for shift in range(RING):
        group = lax.rem(at_ref[0] - shift + RING, RING)
        match = target == iota((target.shape[0], per_group), 1) + group * per_group
        pieces = per_group // sources_ref.shape[1]
        queries = jnp.concatenate(
            [
                sources_ref[shift, :, i * HEAD_DIM : (i + 1) * HEAD_DIM]
                for i in range(pieces)
            ],
            axis=0,
        )
        chosen = chosen + jnp.dot(
            jnp.where(match, 1.0, 0.0).astype(BF16), queries, preferred_element_type=F32
        )
    chosen_ref[...] = chosen.astype(BF16)


def select(at, target, sources, per_group):
    return pl.pallas_call(
        functools.partial(select_kernel, per_group),
        out_shape=jax.ShapeDtypeStruct((target.shape[0], HEAD_DIM), BF16),
        in_specs=[SMEM, VMEM, VMEM],
        out_specs=VMEM,
        compiler_params=params(8),
    )(at, target, sources)


def attend_kernel(*refs):
    count = 2 * RING - 1
    sums, (key_hbm, value_hbm, query_hbm) = refs[:count], refs[count : count + 3]
    out_ref, sums_ref, rows_ref, key_ref, value_ref, query_ref, sum_sems, weight_sems = refs[count + 3 :]
    _, ring, quarter, width = sums_ref.shape
    heads, per_head, per_device, _ = query_ref.shape
    pairs = heads * HEAD_DIM // BLOCK
    copies = [
        pltpu.make_async_copy(ref, sums_ref.at[i], sum_sems.at[i]) for i, ref in enumerate(sums)
    ]
    copies.append(pltpu.make_async_copy(query_hbm, query_ref, sum_sems.at[count]))
    weight_copies = []
    for pair in range(pairs):
        at = pl.ds(pair * BLOCK, BLOCK)
        weight_copies.append(
            [
                pltpu.make_async_copy(hbm.at[:, at], ref.at[:, at], weight_sems.at[i, pair])
                for i, (hbm, ref) in enumerate(((key_hbm, key_ref), (value_hbm, value_ref)))
            ]
        )
    for copy in copies + weight_copies[0]:
        copy.start()
    for more in weight_copies[1:]:
        for copy in more:
            copy.start()
    rows = ring * quarter
    for half, (first, last) in enumerate(((0, RING - 1), (RING - 1, count))):
        for i in range(first, last):
            copies[i].wait()
        summed = sums_ref[first].astype(F32)
        for i in range(first + 1, last):
            summed = summed + sums_ref[i].astype(F32)
        rows_ref[half * rows : (half + 1) * rows] = summed.astype(BF16).reshape(rows, width)
    copies[count].wait()
    many = per_head * per_device
    mine = (
        iota((many, 2 * rows), 0) % per_device // (per_device // 2)
        == iota((many, 2 * rows), 1) // rows
    )
    together = BLOCK // HEAD_DIM
    for pair in range(pairs):
        at = slice(pair * BLOCK, (pair + 1) * BLOCK)
        for copy in weight_copies[pair]:
            copy.wait()
        keys = jnp.dot(rows_ref[...], key_ref[:, at], preferred_element_type=F32)
        values = jnp.dot(rows_ref[...], value_ref[:, at], preferred_element_type=F32).astype(BF16)
        for place in range(together):
            head = pair * together + place
            at = slice(place * HEAD_DIM, (place + 1) * HEAD_DIM)
            key = keys[:, at]
            mean = jnp.mean(key * key, axis=-1, keepdims=True)
            key = (key / jnp.sqrt(mean + epsilon)).astype(BF16)
            query = query_ref[head].reshape(many, HEAD_DIM)
            scores = lax.dot_general(
                query, key, (((1,), (1,)), ((), ())), preferred_element_type=F32
            ) * HEAD_DIM ** (-0.5)
            weights = jnp.where(mine, jnp.exp(scores), 0.0)
            divisor = jnp.sum(weights, axis=-1, keepdims=True)
            numerator = jnp.dot(weights.astype(BF16), values[:, at], preferred_element_type=F32)
            out_ref[head] = (
                jnp.concatenate(
                    [numerator, jnp.broadcast_to(divisor, numerator.shape)], axis=1
                )
                .reshape(per_head, per_device, 2 * HEAD_DIM)
                .astype(BF16)
            )


def attend(sums, key_weight, value_weight, queries):
    shape = sums[0].shape
    _, quarter, width = shape
    heads, per_head, per_device, _ = queries.shape
    columns = key_weight.shape[1]
    return pl.pallas_call(
        attend_kernel,
        out_shape=jax.ShapeDtypeStruct((heads, per_head, per_device, 2 * HEAD_DIM), BF16),
        in_specs=[pl.BlockSpec(memory_space=pl.ANY)] * (len(sums) + 3),
        out_specs=VMEM,
        scratch_shapes=[
            pltpu.VMEM((len(sums),) + shape, BF16),
            pltpu.VMEM((2 * RING * quarter, width), BF16),
            pltpu.VMEM(key_weight.shape, BF16),
            pltpu.VMEM(value_weight.shape, BF16),
            pltpu.VMEM(queries.shape, BF16),
            pltpu.SemaphoreType.DMA((len(sums) + 1,)),
            pltpu.SemaphoreType.DMA((2, columns // BLOCK)),
        ],
        compiler_params=params(ATTEND_MIB),
        cost_estimate=pl.CostEstimate(
            flops=8 * RING * quarter * width * columns,
            bytes_accessed=4 * width * columns,
            transcendentals=0,
        ),
    )(*sums, key_weight, value_weight, queries)


def combine_kernel(at_ref, target_ref, packed_ref, own_ref, one_ref, two_ref, three_ref):
    target = target_ref[...]
    per_group = own_ref.shape[0] - TOTAL_ROWS
    for shift, ref in enumerate((own_ref, one_ref, two_ref, three_ref)):
        group = lax.rem(at_ref[0] + shift, RING)
        match = target == iota((target.shape[0], per_group), 1) + group * per_group
        summed = lax.dot_general(
            jnp.where(match, 1.0, 0.0).astype(BF16),
            packed_ref[...],
            (((0,), (0,)), ((), ())),
            preferred_element_type=F32,
        )
        ref[:per_group] = summed[:, :HEAD_DIM].astype(ref.dtype)
        totals = jnp.zeros((TOTAL_ROWS, HEAD_DIM), F32)
        for row, first in enumerate(range(0, per_group, HEAD_DIM)):
            part = summed[first : first + HEAD_DIM, HEAD_DIM:]
            lane = iota(part.shape, 0) == iota(part.shape, 1)
            part = jnp.sum(jnp.where(lane, part, 0.0), axis=0, keepdims=True)
            totals = jnp.where(iota(totals.shape, 0) == row, part, totals)
        ref[per_group:] = totals.astype(ref.dtype)


def combine(at, target, packed, per_group):
    shape = (per_group + TOTAL_ROWS, HEAD_DIM)
    sent = jax.ShapeDtypeStruct(shape, BF16)
    return pl.pallas_call(
        combine_kernel,
        out_shape=(jax.ShapeDtypeStruct(shape, F32), sent, sent, sent),
        in_specs=[SMEM, VMEM, VMEM],
        out_specs=(VMEM,) * 4,
        compiler_params=params(8),
    )(at, target, packed)


def project_kernel(core, at_ref, own_ref, one_ref, two_ref, three_ref, weight_ref, out_ref):
    summed = own_ref[...]
    for ref in (one_ref, two_ref, three_ref):
        summed = summed + ref[...].astype(F32)
    per_group = summed.shape[0] - TOTAL_ROWS
    attended = []
    for row, first in enumerate(range(0, per_group, HEAD_DIM)):
        part = summed[first : min(first + HEAD_DIM, per_group)]
        totals = jnp.broadcast_to(summed[per_group + row : per_group + row + 1], part.shape)
        lane = iota(part.shape, 0) == iota(part.shape, 1)
        divisor = jnp.sum(jnp.where(lane, totals, 0.0), axis=1, keepdims=True)
        attended.append(part / jnp.where(divisor > 0.0, divisor, 1.0))
    attended = jnp.concatenate(attended, axis=0)
    half = per_group // 2
    attended = jnp.concatenate([attended[:half], attended[half:]], axis=1).astype(BF16)
    here = at_ref[1]
    z_at, y_at, core_at = here // (RING * CORES), here // CORES % RING, here % CORES
    column = lax.rem(core_at + core, CORES)
    for z in range(RING):
        for y in range(RING):
            block = (
                lax.rem(z_at + z, RING) * RING + lax.rem(y_at + y, RING)
            ) * CORES + column
            at = pl.ds(pl.multiple_of(block * BLOCK, BLOCK), BLOCK)
            out_ref[z, y] = jnp.dot(
                attended, weight_ref[:, at], preferred_element_type=F32
            ).astype(BF16)


def project(at, own, received, weight, core):
    depth, columns = weight.shape
    rows = (own.shape[0] - TOTAL_ROWS) // 2
    return pl.pallas_call(
        functools.partial(project_kernel, core),
        out_shape=jax.ShapeDtypeStruct((RING, RING, rows, BLOCK), BF16),
        in_specs=[SMEM] + [VMEM] * 5,
        out_specs=VMEM,
        compiler_params=params(8),
        cost_estimate=pl.CostEstimate(
            flops=rows * depth * columns, bytes_accessed=2 * depth * columns, transcendentals=0
        ),
    )(at, own, *received, weight)


def first_sum_kernel(kept_ref, got_ref, own_ref, one_ref, two_ref, three_ref):
    for shift, ref in enumerate((own_ref, one_ref, two_ref, three_ref)):
        ref[...] = (kept_ref[shift].astype(F32) + got_ref[shift].astype(F32)).astype(ref.dtype)


def first_sum(kept, got):
    sent = jax.ShapeDtypeStruct(kept.shape[1:], BF16)
    return pl.pallas_call(
        first_sum_kernel,
        out_shape=(jax.ShapeDtypeStruct(kept.shape[1:], F32), sent, sent, sent),
        in_specs=[VMEM, VMEM],
        out_specs=(VMEM,) * 4,
        compiler_params=params(8),
    )(kept, got)


def second_sum_kernel(kept_ref, a_ref, b_ref, c_ref, own_ref, one_ref, two_ref, three_ref):
    for shift, ref in enumerate((own_ref, one_ref, two_ref, three_ref)):
        summed = kept_ref[shift]
        for got in (a_ref, b_ref, c_ref):
            summed = summed + got[shift].astype(F32)
        ref[...] = summed.astype(ref.dtype)


def second_sum(kept, got):
    sent = jax.ShapeDtypeStruct(kept.shape[1:], BF16)
    return pl.pallas_call(
        second_sum_kernel,
        out_shape=(jax.ShapeDtypeStruct(kept.shape[1:], F32), sent, sent, sent),
        in_specs=[VMEM] * 4,
        out_specs=(VMEM,) * 4,
        compiler_params=params(8),
    )(kept, *got)


def last_sum_kernel(kept_ref, a_ref, b_ref, c_ref, residual_ref, out_ref):
    summed = kept_ref[...]
    for got in (a_ref, b_ref, c_ref):
        summed = summed + got[...].astype(F32)
    out_ref[...] = (residual_ref[...].astype(F32) + summed.reshape(out_ref.shape)).astype(BF16)


def last_sum(kept, got, residual):
    return pl.pallas_call(
        last_sum_kernel,
        out_shape=jax.ShapeDtypeStruct(residual.shape, BF16),
        in_specs=[VMEM] * 5,
        out_specs=VMEM,
        compiler_params=params(8),
    )(kept, *got, residual)


def body(
    patches,
    enc_tiles,
    req_tiles,
    req_owner,
    fc1_weight,
    fc2_weight,
    key_weight,
    value_weight,
    query_weight,
    out_weight,
    text_hidden,
):
    capacity = patches.shape[0]
    devices = lax.axis_size("dev")
    local_heads = HEADS // devices
    slots, steps, model_width = text_hidden.shape
    dev_at = lax.axis_index("dev")
    at = jnp.stack([lax.axis_index("pool"), dev_at]).astype(jnp.int32)
    halves = capacity // RING

    own = [normalize(at, patches), second_half(at, text_hidden, query_weight, patches)]
    sources = [[rows] + [pool_shift(rows, s) for s in range(1, RING)] for rows in own]
    held = hold(fc1_weight, fc2_weight, sources[0][0])
    target = tables(
        at,
        enc_tiles.reshape(1, -1),
        req_tiles.reshape(1, -1),
        req_owner,
        slots,
        steps,
        local_heads,
        capacity,
        sources[0][0],
    )
    sums, queries = [], None
    for i in range(halves):
        total, *messages = feed_forward(
            at, patches, sources[i], fc1_weight, fc2_weight, i, (held, target)
        )
        queries = messages[-1]
        if i == 0:
            near = pair_sum(messages[0], pool_shift(messages[1], 1))
            sums += [total, pool_shift(messages[2], -1), pool_shift(near, 1)]
        else:
            sums += [total] + [pool_shift(messages[s - 1], s) for s in range(1, RING)]
    chosen = select(at, target, queries, local_heads * slots * steps)
    per_device = halves * local_heads * steps
    tile_queries = lax.all_to_all(
        chosen.reshape(devices, per_device, HEAD_DIM), "dev", split_axis=0, concat_axis=0, tiled=True
    ).reshape(KV_HEADS, devices // KV_HEADS, per_device, HEAD_DIM)
    packed = attend(sums, key_weight, value_weight, tile_queries)
    packed = lax.all_to_all(
        packed.reshape(devices, per_device, 2 * HEAD_DIM),
        "dev",
        split_axis=0,
        concat_axis=0,
        tiled=True,
    ).reshape(devices * per_device, 2 * HEAD_DIM)
    summed, *messages = combine(at, target, packed, local_heads * slots * steps)
    received = [pool_shift(messages[s - 1], s) for s in range(1, RING)]

    away = dev_shift(project(at, summed, received, out_weight, 1), 0, 0, 1)
    kept = project(at, summed, received, out_weight, 0)
    kept, *messages = first_sum(kept, away)
    received = [dev_shift(messages[s - 1], s, 0, 0) for s in range(1, RING)]
    kept, *messages = second_sum(kept, received)
    received = [dev_shift(messages[s - 1], 0, s, 0) for s in range(1, RING)]
    width_out = model_width // devices
    residual = lax.dynamic_slice_in_dim(text_hidden, dev_at * width_out, width_out, 2)
    return last_sum(kept, received, residual)


def solution(mesh):
    return jax.shard_map(
        body,
        mesh=mesh,
        in_specs=(
            P("dev", "pool", None),
            P(),
            P(),
            P(),
            P(None, "pool"),
            P("pool", None),
            P(),
            P(),
            P(None, "dev"),
            P("dev", None),
            P("pool", None, None),
        ),
        out_specs=P("pool", None, "dev"),
        check_vma=False,
    )
```
